256 devices in a mesh: rows: 64 (over z_lo, y, x), cols: 4 (over z_hi, core).
Axes of the slice: x: 4, y: 4, z: 8 (z_hi: 2, z_lo: 4; z = z_hi * 4 + z_lo), core: 2. Of those that a mesh axis runs over, the one named last changes fastest.
Arguments:
- elevation: float32 [4096, 4096], P(('rows', 'cols')), may hold values from -2.4 to 2.4
- potential: float32 [4096, 4096], P(('rows', 'cols')), may hold values from -6 to 6
- elevation_cot: float32 [4096, 4096], P(('rows', 'cols')), may hold values from -6 to 6
- potential_cot: float32 [4096, 4096], P(('rows', 'cols')), may hold values from -6 to 6
Outputs:
- elevation_grad: float32 [4096, 4096], P(('rows', 'cols'))
- potential_grad: float32 [4096, 4096], P(('rows', 'cols'))
The draws below stay inside these ranges and needn't reach their ends.
All inputs are finite; a program needn't handle non-finite values.
Results may differ from the reference program's by a relative error of at most 0.00011.
Values sent between devices are 32-bit elements; how exact they have to be, the bound alone decides.
No kernel may reach another device: no remote copies, remote signals or barrier semaphores. Data moves between devices by JAX's collectives and lax.ppermute only.
A program may use at most 128 MiB of HBM per device.

```python
import jax
import jax.numpy as jnp

NX = 4096
NY = 4096


def block_levels(key, shape, pieces, low, largest):
    def one(dim, blocks):
        heights = jax.random.uniform(jax.random.fold_in(jax.random.fold_in(key, 6), dim), (blocks,), jnp.float32, low / len(pieces), largest / len(pieces))
        return jnp.repeat(jnp.exp(heights), shape[dim] // blocks).reshape((-1,) + (1,) * (len(shape) - dim - 1))

    factor_of = one(*pieces[0])
    for cut in pieces[1:]:
        factor_of = factor_of * one(*cut)
    return factor_of


def noise(own_key, dims, scale, limit, shards=(), kind=jnp.bfloat16):
    entries = jax.random.normal(own_key, dims, jnp.float32) * scale
    if len(shards) > 0:
        entries = block_levels(own_key, dims, shards, -0.22, 0.18) * entries
    return jnp.clip(entries, min=-limit, max=limit).astype(kind)


def setup_inputs(seed: int = 0) -> dict:
    key_of = jax.random.split(jax.random.key(seed), 5)
    elevation = noise(key_of[0], (NX, NY), 0.4, 2.4, ((0, 256),), jnp.float32)
    potential = noise(key_of[1], (NX, NY), 1.0, 6.0, ((0, 256),), jnp.float32)
    elevation_cot = noise(key_of[2], (NX, NY), 1.0, 6.0, ((0, 256),), jnp.float32)
    potential_cot = noise(key_of[3], (NX, NY), 1.0, 6.0, ((0, 256),), jnp.float32)
    return dict(elevation=elevation, potential=potential, elevation_cot=elevation_cot, potential_cot=potential_cot)


stiffness = 0.05
section_step = 0.25

def signed_modes(length):
    mode_list = jnp.arange(length, dtype=jnp.int32)
    return jnp.where(mode_list < length // 2, mode_list, mode_list - length)

def filtered_op(surface, multiplier, rotate):
    spectrum = jnp.fft.fft2(surface) * multiplier
    if rotate:
        spectrum = spectrum * 1j
    return jnp.real(jnp.fft.ifft2(spectrum))

def section_map(elevation, potential):
    mode_x = signed_modes(NX)[:, None]
    mode_y = signed_modes(NY)[None, :]
    wave_x = 2.0 * jnp.pi / NX * mode_x.astype(jnp.float32)
    wave_y = 2.0 * jnp.pi / NY * mode_y.astype(jnp.float32)
    keep_mask = ((jnp.abs(mode_x) < NX // 4) & (jnp.abs(mode_y) < NY // 4)).astype(jnp.float32)
    magnitude = jnp.sqrt(wave_x * wave_x + wave_y * wave_y)

    def lift_by(surface, exponent):
        return filtered_op(surface, keep_mask * magnitude ** exponent, False)
    slope_x = filtered_op(elevation, keep_mask * wave_x, True)
    slope_y = filtered_op(elevation, keep_mask * wave_y, True)
    flow_x = filtered_op(potential, keep_mask * wave_x, True)
    flow_y = filtered_op(potential, keep_mask * wave_y, True)
    bend = lift_by(elevation, 4)
    power_one = elevation
    power_two = elevation * elevation / 2.0
    power_three = power_two * elevation / 3.0
    powers = {1: 1.0, 2: power_one, 3: power_two, 4: power_three}
    lifted = {}
    for degree in range(1, 5):
        lifted[1, degree] = lift_by(potential, degree)
    order_two = -power_one * lifted[1, 1]
    for degree in range(1, 4):
        lifted[2, degree] = lift_by(order_two, degree)
    order_three = -power_one * lifted[2, 1] - power_two * lifted[1, 2]
    for degree in range(1, 3):
        lifted[3, degree] = lift_by(order_three, degree)
    order_four = -power_one * lifted[3, 1] - power_two * lifted[2, 2] - power_three * lifted[1, 3]
    lifted[4, 1] = lift_by(order_four, 1)
    vertical = jnp.zeros_like(elevation)
    for order_index in range(1, 5):
        for degree in range(1, 6 - order_index):
            vertical = vertical + powers[degree] * lifted[order_index, degree]
    steepness = 1.0 + slope_x * slope_x + slope_y * slope_y
    rate_eta = steepness * vertical - (slope_x * flow_x + slope_y * flow_y)
    rate_phi = -elevation - stiffness * bend - 0.5 * (flow_x * flow_x + flow_y * flow_y) + 0.5 * steepness * vertical * vertical
    return (elevation + section_step * rate_eta, potential + section_step * rate_phi)

def reference(elevation, potential, elevation_cot, potential_cot):
    outputs, pullback = jax.vjp(section_map, elevation, potential)
    elevation_grad, potential_grad = pullback((elevation_cot, potential_cot))
    return (elevation_grad, potential_grad)
```

```python
import functools

import jax
import jax.numpy as jnp
import numpy as np
from jax import lax
from jax.experimental import pallas as pl
from jax.experimental.pallas import tpu as pltpu
from jax.sharding import PartitionSpec as P

stiffness = 0.05
section_step = 0.25
side = 4096
devices = 256
local_rows = 16
radix = 16
fine = 256
kept_y = 64
kept_a = np.array([0, 1, 2, 3, 12, 13, 14, 15])
mesh_axes = ("rows", "cols")


def split_table(table):
    table = table.astype(np.float32)
    high = table.astype(jnp.bfloat16)
    low = (table - high.astype(np.float32)).astype(jnp.bfloat16)
    return np.stack((high, low), 0)


@functools.lru_cache(maxsize=None)
def tables():
    two_pi = 2.0 * np.pi
    eye_j = np.eye(local_rows)
    residue = np.arange(radix)
    angle = two_pi * np.outer(np.arange(radix), residue) / radix
    parts = np.stack((np.cos(angle), -np.sin(angle)), 0).reshape(2, radix, 4, 4)
    right_y = np.einsum("cthl,jk->tjhckl", parts, eye_j).reshape(radix * local_rows, 512)
    angle = two_pi * np.outer(np.arange(fine), residue) / side
    cosine = np.cos(angle).reshape(fine, 4, 1, 1, 4)
    sine = np.sin(angle).reshape(fine, 4, 1, 1, 4)
    signs = np.array([1.0, -1.0]).reshape(1, 1, 2, 1, 1)
    full = (fine, 4, 2, local_rows, 4)
    twist_y = np.stack(
        (np.broadcast_to(cosine, full).reshape(fine, 512), np.broadcast_to(sine * signs, full).reshape(fine, 512)), 0
    )
    angle = two_pi * np.outer(np.arange(kept_y), np.arange(fine)) / fine
    left_y = np.concatenate((np.cos(angle), np.sin(angle)), 0)
    left_y_back = left_y.T
    angle = two_pi * np.outer(np.arange(fine), np.arange(fine)) / fine
    left_x = np.concatenate((np.cos(angle), np.sin(angle)), 0)
    angle = two_pi * np.outer(np.arange(fine), np.arange(local_rows)) / side
    full = (fine, 2, local_rows, 4)
    signs = np.array([1.0, -1.0]).reshape(1, 2, 1, 1)
    twist_x = np.stack(
        (
            np.broadcast_to(np.cos(angle)[:, None, :, None], full).reshape(fine, 128),
            np.broadcast_to(np.sin(angle)[:, None, :, None] * signs, full).reshape(fine, 128),
        ),
        0,
    )
    angle = two_pi * np.outer(np.arange(local_rows), kept_a) / radix
    cosine, sine = (np.cos(angle), np.sin(angle))
    eye_q = np.eye(4)
    forward = np.array([[cosine, -sine], [sine, cosine]])
    right_x = np.einsum("cdja,qp->cjqdap", forward, eye_q).reshape(128, 64)
    turned = np.array([[-sine, cosine], [-cosine, -sine]])
    right_x_back = right_x.T
    right_x_turn = np.einsum("cdja,qp->caqdjp", turned, eye_q).reshape(64, 128)
    return dict(
        right_y=split_table(right_y),
        right_y_back=split_table(right_y.T),
        left_y=split_table(left_y),
        left_y_back=split_table(left_y_back),
        twist_y=twist_y.astype(np.float32),
        left_x=split_table(left_x),
        right_x=split_table(right_x),
        right_x_back=split_table(right_x_back),
        right_x_turn=split_table(right_x_turn),
        twist_x=twist_x.astype(np.float32),
    )


y_names = ("right_y", "right_y_back", "left_y", "left_y_back", "twist_y")
x_names = ("left_x", "right_x", "right_x_back", "right_x_turn", "twist_x")


def parted(values):
    high = values.astype(jnp.bfloat16)
    return (high, (values - high.astype(jnp.float32)).astype(jnp.bfloat16))


def product(first, second):
    return jnp.dot(first, second, preferred_element_type=jnp.float32)


def left_times(table_ref, values):
    high, low = parted(values)
    return product(table_ref[0], high) + (product(table_ref[1], high) + product(table_ref[0], low))


def times_right(values, table_ref):
    high, low = parted(values)
    return product(high, table_ref[0]) + (product(low, table_ref[0]) + product(high, table_ref[1]))


def swapped(values):
    pieces = [
        pltpu.roll(values[:, start : start + 128], 64, 1) for start in range(0, values.shape[1], 128)
    ]
    return pieces[0] if len(pieces) == 1 else jnp.concatenate(pieces, 1)


def half_signs(shape):
    lane = lax.broadcasted_iota(jnp.int32, shape, 1)
    return jnp.where(lane % 128 < 64, 1.0, -1.0).astype(jnp.float32)


def y_forward(tab, field, message_ref, slot, count):
    values = times_right(field, tab["right_y"])
    values = values * tab["twist_y"][0] + swapped(values) * tab["twist_y"][1]
    both = left_times(tab["left_y"], values)
    turned = swapped(both[kept_y:])
    values = both[:kept_y] + turned * half_signs(turned.shape)
    for part in range(4):
        message_ref[pl.ds(part * count + slot, kept_y, stride=4 * count), :] = values[
            :, part * 128 : part * 128 + 128
        ]


def y_inverse(tab, arrived_ref, slot, count):
    values = jnp.concatenate(
        [arrived_ref[pl.ds(part * count + slot, kept_y, stride=4 * count), :] for part in range(4)], 1
    )
    turned = swapped(values)
    stacked = jnp.concatenate((values, turned * -half_signs(turned.shape)), 0)
    values = left_times(tab["left_y_back"], stacked)
    values = values * tab["twist_y"][0] - swapped(values) * tab["twist_y"][1]
    return times_right(values, tab["right_y_back"])


def x_forward(tab, arrived_ref, slot, count):
    values = arrived_ref[pl.ds(slot, fine, stride=count), :] if count > 1 else arrived_ref[...]
    both = left_times(tab["left_x"], values)
    turned = swapped(both[fine:])
    values = both[:fine] + turned * half_signs(turned.shape)
    values = values * tab["twist_x"][0] + swapped(values) * tab["twist_x"][1]
    return times_right(values, tab["right_x"])


def x_inverse(tab, straight, turned_part, message_ref, slot, count):
    if straight is None:
        values = times_right(turned_part, tab["right_x_turn"])
    else:
        values = times_right(straight, tab["right_x_back"])
        if turned_part is not None:
            values = values + times_right(turned_part, tab["right_x_turn"])
    values = values * tab["twist_x"][0] - swapped(values) * tab["twist_x"][1]
    both = left_times(tab["left_x"], values)
    turned = swapped(both[fine:])
    values = both[:fine] - turned * half_signs(turned.shape)
    put(message_ref, values, slot, count)


def put(message_ref, values, slot, count):
    if count > 1:
        message_ref[pl.ds(slot, fine, stride=count), :] = values
    else:
        message_ref[...] = values


def message(count):
    return jax.ShapeDtypeStruct((devices * count, 128), jnp.float32)


field_shape = jax.ShapeDtypeStruct((256, 256), jnp.float32)
spectrum_shape = jax.ShapeDtypeStruct((fine, 64), jnp.float32)


def run(body, names, inputs, outputs, flops):
    table_values = [jnp.asarray(tables()[name]) for name in names]

    def kernel(*refs):
        tab = dict(zip(names, refs[: len(names)]))
        ins = refs[len(names) : len(names) + len(inputs)]
        outs = refs[len(names) + len(inputs) :]
        body(tab, ins, outs)

    whole = pl.BlockSpec(memory_space=pltpu.VMEM)
    moved = sum(4 * int(np.prod(a.shape)) for a in list(inputs) + list(outputs))
    return pl.pallas_call(
        kernel,
        out_shape=list(outputs),
        in_specs=[whole] * (len(names) + len(inputs)),
        out_specs=[whole] * len(outputs),
        compiler_params=pltpu.CompilerParams(vmem_limit_bytes=32 * 1024 * 1024),
        cost_estimate=pl.CostEstimate(flops=int(flops * 6e8), bytes_accessed=int(moved), transcendentals=0),
    )(*table_values, *inputs)


def exchange(values):
    count = values.shape[0] // devices
    values = values.reshape(devices, count, 128)
    values = lax.all_to_all(values, mesh_axes, split_axis=0, concat_axis=0, tiled=True)
    return values.reshape(devices * count, 128)


def gather_rows(block):
    pieces = [block[:, start : start + 256] for start in range(0, side, 256)]
    return jnp.concatenate(pieces, 0).T


def scatter_rows(out_ref, field):
    turned = field.T
    for part in range(radix):
        out_ref[:, part * 256 : part * 256 + 256] = turned[part * local_rows : (part + 1) * local_rows, :]


def wave_tables():
    own = lax.axis_index("rows") * lax.axis_size("cols") + lax.axis_index("cols")
    lane = jnp.arange(64, dtype=jnp.int32)
    digit = (lane // 4) % 8
    mode_y = 4 * own + lane % 4
    row = jnp.arange(fine, dtype=jnp.int32)
    mode_x = 256 * jnp.where(digit < 4, digit, digit - 8)[None, :] + row[:, None]
    wave_x = (2.0 * jnp.pi / side) * mode_x.astype(jnp.float32)
    wave_y = jnp.broadcast_to(((2.0 * jnp.pi / side) * mode_y.astype(jnp.float32))[None, :], wave_x.shape)
    weight = jnp.where(mode_y == 0, 1.0, 2.0)[None, :] / (side * side)
    keep = jnp.where(jnp.abs(mode_x) < side // 4, weight, 0.0).astype(jnp.float32)
    magnitude = jnp.sqrt(wave_x * wave_x + wave_y * wave_y)
    return jnp.stack((keep, magnitude, wave_x, wave_y), 0)


def per_device(elevation, potential, elevation_cot, potential_cot):
    waves = wave_tables()

    def start(tab, ins, outs):
        surface = gather_rows(ins[0][...])
        outs[0][...] = surface
        y_forward(tab, gather_rows(ins[1][...]), outs[1], 1, 2)
        y_forward(tab, surface, outs[1], 0, 2)

    elev, sent = run(start, y_names, (elevation, potential), (field_shape, message(2)), 2)
    first = exchange(sent)

    def cotangents(tab, ins, outs):
        outs[0][...] = section_step * gather_rows(ins[0][...])
        rate = section_step * gather_rows(ins[1][...])
        outs[1][...] = rate
        y_forward(tab, -stiffness * rate, outs[2], 0, 1)

    rate_elev, rate_pot, bend_sent = run(
        cotangents, y_names, (elevation_cot, potential_cot), (field_shape, field_shape, message(1)), 1
    )

    def second(tab, ins, outs):
        spec = x_forward(tab, ins[0], 1, 2)
        outs[1][...] = spec * ins[1][0]
        spec = spec * ins[1][0]
        for degree in range(4):
            spec = spec * ins[1][1]
            x_inverse(tab, spec, None, outs[0], degree, 4)

    sent, pot_spec = run(second, x_names, (first, waves), (message(4), spectrum_shape), 2)
    lifts = exchange(sent)

    def slopes(tab, ins, outs):
        spec = x_forward(tab, ins[0], 0, 2) * ins[2][0]
        x_inverse(tab, None, spec * ins[2][2], outs[0], 0, 1)
        x_inverse(tab, None, spec * ins[2][3], outs[1], 0, 1)
        spec = ins[1][...]
        x_inverse(tab, None, spec * ins[2][2], outs[2], 0, 1)
        x_inverse(tab, None, spec * ins[2][3], outs[3], 0, 1)

    slope_x_sent, slope_y_sent, flow_x_sent, flow_y_sent = run(
        slopes, x_names, (first, pot_spec, waves), (message(1),) * 4, 2
    )

    def third(tab, ins, outs):
        lifted = y_inverse(tab, ins[0], 0, 4)
        outs[1][...] = lifted
        y_forward(tab, -ins[1][...] * lifted, outs[0], 0, 2)
        put(outs[0], ins[2][...], 1, 2)

    sent, lift_11 = run(third, y_names, (lifts, elev, bend_sent), (message(2), field_shape), 2)
    arrived = exchange(sent)

    def inverse_of(slots, count):
        def body(tab, ins, outs):
            for place, slot in enumerate(slots):
                outs[place][...] = y_inverse(tab, ins[0], slot, count)

        return body

    lift_12, lift_13, lift_14 = run(inverse_of((1, 2, 3), 4), y_names, (lifts,), (field_shape,) * 3, 3)

    def fourth(tab, ins, outs):
        spec = x_forward(tab, ins[0], 0, 2) * ins[1][0]
        for degree in range(3):
            spec = spec * ins[1][1]
            x_inverse(tab, spec, None, outs[0], degree, 4)
        put(outs[0], ins[2][...], 3, 4)

    (sent,) = run(fourth, x_names, (arrived, waves, slope_x_sent), (message(4),), 2)

    def spectra_of(slots, count):
        def body(tab, ins, outs):
            for place, slot in enumerate(slots):
                outs[place][...] = x_forward(tab, ins[0], slot, count) * ins[1][0]

        return body

    (bend_spec,) = run(spectra_of((1,), 2), x_names, (arrived, waves), (spectrum_shape,), 1)
    arrived = exchange(sent)

    def fifth(tab, ins, outs):
        lifted = y_inverse(tab, ins[0], 0, 4)
        outs[1][...] = lifted
        surface = ins[1][...]
        y_forward(tab, -surface * lifted - (surface * surface / 2.0) * ins[2][...], outs[0], 0, 1)

    sent, lift_21 = run(fifth, y_names, (arrived, elev, lift_12), (message(1), field_shape), 2)
    lift_22, lift_23, slope_x = run(inverse_of((1, 2, 3), 4), y_names, (arrived,), (field_shape,) * 3, 3)
    arrived = exchange(sent)

    def sixth(tab, ins, outs):
        spec = x_forward(tab, ins[0], 0, 1) * ins[1][0]
        for degree in range(2):
            spec = spec * ins[1][1]
            x_inverse(tab, spec, None, outs[0], degree, 4)
        put(outs[0], ins[2][...], 2, 4)
        put(outs[0], ins[3][...], 3, 4)

    (sent,) = run(sixth, x_names, (arrived, waves, slope_y_sent, flow_x_sent), (message(4),), 2)
    arrived = exchange(sent)

    def seventh(tab, ins, outs):
        lifted = y_inverse(tab, ins[0], 0, 4)
        outs[1][...] = lifted
        surface = ins[1][...]
        square = surface * surface / 2.0
        cube = square * surface / 3.0
        y_forward(tab, -surface * lifted - square * ins[2][...] - cube * ins[3][...], outs[0], 0, 1)

    sent, lift_31 = run(seventh, y_names, (arrived, elev, lift_22, lift_13), (message(1), field_shape), 2)
    lift_32, slope_y, flow_x = run(inverse_of((1, 2, 3), 4), y_names, (arrived,), (field_shape,) * 3, 3)
    arrived = exchange(sent)

    def eighth(tab, ins, outs):
        spec = x_forward(tab, ins[0], 0, 1) * (ins[1][0] * ins[1][1])
        x_inverse(tab, spec, None, outs[0], 0, 2)
        put(outs[0], ins[2][...], 1, 2)

    (sent,) = run(eighth, x_names, (arrived, waves, flow_y_sent), (message(2),), 1)
    arrived = exchange(sent)

    square = elev * elev / 2.0
    cube = square * elev / 3.0
    partial = (
        lift_11
        + lift_21
        + lift_31
        + elev * (lift_12 + lift_22 + lift_32)
        + square * (lift_13 + lift_23)
        + cube * lift_14
    )
    growth = lift_12 + lift_22 + lift_32 + elev * (lift_13 + lift_23) + square * lift_14
    steepness = 1.0 + slope_x * slope_x + slope_y * slope_y

    def ninth(tab, ins, outs):
        vertical = ins[1][...] + y_inverse(tab, ins[0], 0, 2)
        vertical_cot = ins[2][...] * (ins[3][...] + vertical * ins[4][...])
        outs[1][...] = vertical
        outs[2][...] = vertical_cot
        y_forward(tab, vertical_cot, outs[0], 0, 2)
        y_forward(tab, ins[5][...] * vertical_cot, outs[0], 1, 2)

    sent, vertical, vertical_cot = run(
        ninth,
        y_names,
        (arrived, partial, steepness, rate_elev, rate_pot, elev),
        (message(2), field_shape, field_shape),
        3,
    )
    (flow_y,) = run(inverse_of((1,), 2), y_names, (arrived,), (field_shape,), 1)
    arrived = exchange(sent)
    steep_cot = vertical * rate_elev + 0.5 * vertical * vertical * rate_pot

    def forward_all(tab, ins, outs):
        for place in range(len(ins)):
            y_forward(tab, ins[place][...], outs[place], 0, 1)

    def sends_of(*fields):
        return run(forward_all, y_names, fields, (message(1),) * len(fields), len(fields))

    square_cot_sent, cube_cot_sent = sends_of(square * vertical_cot, cube * vertical_cot)
    slope_x_cot, slope_y_cot = sends_of(
        -flow_x * rate_elev + 2.0 * slope_x * steep_cot, -flow_y * rate_elev + 2.0 * slope_y * steep_cot
    )
    flow_x_cot, flow_y_cot = sends_of(
        -slope_x * rate_elev - flow_x * rate_pot, -slope_y * rate_elev - flow_y * rate_pot
    )

    def tenth(tab, ins, outs):
        spec = x_forward(tab, ins[0], 0, 2) * ins[1][0]
        outs[1][...] = spec
        x_inverse(tab, spec * ins[1][1], None, outs[0], 0, 1)

    sent, cot_spec = run(tenth, x_names, (arrived, waves), (message(1), spectrum_shape), 1)
    (elev_cot_spec,) = run(spectra_of((1,), 2), x_names, (arrived, waves), (spectrum_shape,), 1)
    arrived = exchange(sent)

    def eleventh(tab, ins, outs):
        lifted = y_inverse(tab, ins[0], 0, 1)
        outs[1][...] = lifted
        surface = ins[1][...]
        y_forward(tab, surface * lifted, outs[0], 0, 4)
        y_forward(tab, (surface * surface / 2.0) * lifted, outs[0], 1, 4)
        put(outs[0], ins[2][...], 2, 4)
        put(outs[0], ins[3][...], 3, 4)

    sent, fourth_cot = run(
        eleventh, y_names, (arrived, elev, square_cot_sent, cube_cot_sent), (message(4), field_shape), 3
    )
    (cube_fourth_sent,) = sends_of(cube * fourth_cot)
    arrived = exchange(sent)

    def twelfth(tab, ins, outs):
        spec = x_forward(tab, ins[0], 0, 4) * ins[1][0]
        spec = ins[1][1] * ((ins[2][...] - spec) + ins[1][1] * ins[3][...])
        x_inverse(tab, spec, None, outs[0], 0, 1)

    (sent,) = run(twelfth, x_names, (arrived, waves, cot_spec, elev_cot_spec), (message(1),), 1)
    square_fourth_spec, square_cot_spec, cube_cot_spec = run(
        spectra_of((1, 2, 3), 4), x_names, (arrived, waves), (spectrum_shape,) * 3, 1
    )
    arrived = exchange(sent)

    def thirteenth(tab, ins, outs):
        lifted = y_inverse(tab, ins[0], 0, 1)
        outs[1][...] = lifted
        y_forward(tab, ins[1][...] * lifted, outs[0], 0, 4)
        for slot in range(1, 4):
            put(outs[0], ins[1 + slot][...], slot, 4)

    sent, third_cot = run(
        thirteenth,
        y_names,
        (arrived, elev, cube_fourth_sent, slope_x_cot, slope_y_cot),
        (message(4), field_shape),
        2,
    )
    (square_third_sent,) = sends_of(square * third_cot)
    arrived = exchange(sent)

    def fourteenth(tab, ins, outs):
        wave = ins[1][1]
        spec = x_forward(tab, ins[0], 0, 4) * ins[1][0]
        spec = wave * (
            (ins[2][...] - spec) + wave * ((ins[3][...] - ins[4][...]) + wave * ins[5][...])
        )
        x_inverse(tab, spec, None, outs[0], 0, 1)

    (sent,) = run(
        fourteenth,
        x_names,
        (arrived, waves, cot_spec, elev_cot_spec, square_fourth_spec, square_cot_spec),
        (message(1),),
        1,
    )

    def gathered(tab, ins, outs):
        wave = ins[1][1]
        cube_fourth = x_forward(tab, ins[0], 1, 4) * ins[1][0]
        outs[0][...] = wave * (
            ins[2][...]
            + wave * (ins[3][...] + wave * ((ins[4][...] - cube_fourth) + wave * ins[5][...]))
        )
        slope_x_spec = x_forward(tab, ins[0], 2, 4) * ins[1][0]
        slope_y_spec = x_forward(tab, ins[0], 3, 4) * ins[1][0]
        outs[1][...] = -(ins[1][2] * slope_x_spec + ins[1][3] * slope_y_spec)
        outs[2][...] = ins[6][...] * (wave * wave) * (wave * wave)

    pot_part, elev_turn, elev_part = run(
        gathered,
        x_names,
        (arrived, waves, cot_spec, elev_cot_spec, square_cot_spec, cube_cot_spec, bend_spec),
        (spectrum_shape,) * 3,
        1,
    )
    arrived = exchange(sent)

    def fifteenth(tab, ins, outs):
        lifted = y_inverse(tab, ins[0], 0, 1)
        outs[1][...] = lifted
        y_forward(tab, ins[1][...] * lifted, outs[0], 0, 4)
        for slot in range(1, 4):
            put(outs[0], ins[1 + slot][...], slot, 4)

    sent, second_cot = run(
        fifteenth,
        y_names,
        (arrived, elev, square_third_sent, flow_x_cot, flow_y_cot),
        (message(4), field_shape),
        2,
    )
    arrived = exchange(sent)

    def elevation_side(tab, ins, outs):
        x_inverse(tab, ins[0][...], ins[1][...], outs[0], 0, 1)

    (elev_sent,) = run(elevation_side, x_names, (elev_part, elev_turn), (message(1),), 1)

    def sixteenth(tab, ins, outs):
        wave = ins[1][1]
        keep = ins[1][0]
        first_part = x_forward(tab, ins[0], 0, 4) * keep
        second_part = x_forward(tab, ins[0], 1, 4) * keep
        flow_part = x_forward(tab, ins[0], 2, 4) * ins[1][2] + x_forward(tab, ins[0], 3, 4) * ins[1][3]
        straight = ins[2][...] - wave * (first_part + wave * second_part)
        x_inverse(tab, straight, -flow_part * keep, outs[0], 1, 2)
        put(outs[0], ins[3][...], 0, 2)

    (sent,) = run(sixteenth, x_names, (arrived, waves, pot_part, elev_sent), (message(2),), 2)
    arrived = exchange(sent)

    grad = (
        vertical_cot * growth
        - (lift_31 + elev * lift_22 + square * lift_13) * fourth_cot
        - (lift_21 + elev * lift_12) * third_cot
        - lift_11 * second_cot
        - rate_pot
    )

    def finish(tab, ins, outs):
        scatter_rows(outs[0], ins[1][...] + y_inverse(tab, ins[0], 0, 2))
        outs[0][...] = outs[0][...] + ins[2][...]
        scatter_rows(outs[1], y_inverse(tab, ins[0], 1, 2))
        outs[1][...] = outs[1][...] + ins[3][...]

    block = jax.ShapeDtypeStruct(elevation.shape, jnp.float32)
    elevation_grad, potential_grad = run(
        finish, y_names, (arrived, grad, elevation_cot, potential_cot), (block, block), 2
    )
    return (elevation_grad, potential_grad)


def solution(mesh):
    spec = P(mesh_axes, None)
    return jax.shard_map(
        per_device, mesh=mesh, in_specs=(spec,) * 4, out_specs=(spec, spec), check_vma=False
    )
```

```python
import functools

import jax
import jax.numpy as jnp
import numpy as np
from jax import lax
from jax.experimental import pallas as pl
from jax.experimental.pallas import tpu as pltpu
from jax.sharding import PartitionSpec as P

stiffness = 0.05
section_step = 0.25
side = 4096
devices = 256
local_rows = 16
radix = 16
fine = 256
kept_y = 64
kept_a = np.array([0, 1, 2, 3, 12, 13, 14, 15])
mesh_axes = ("rows", "cols")


def split_table(table):
    table = table.astype(np.float32)
    high = table.astype(jnp.bfloat16)
    low = (table - high.astype(np.float32)).astype(jnp.bfloat16)
    return np.stack((high, low), 0)


@functools.lru_cache(maxsize=None)
def tables():
    two_pi = 2.0 * np.pi
    eye_j = np.eye(local_rows)
    residue = np.arange(radix)
    angle = two_pi * np.outer(np.arange(radix), residue) / radix
    parts = np.stack((np.cos(angle), -np.sin(angle)), 0).reshape(2, radix, 4, 4)
    right_y = np.einsum("cthl,jk->tjhckl", parts, eye_j).reshape(radix * local_rows, 512)
    angle = two_pi * np.outer(np.arange(fine), residue) / side
    cosine = np.cos(angle).reshape(fine, 4, 1, 1, 4)
    sine = np.sin(angle).reshape(fine, 4, 1, 1, 4)
    signs = np.array([1.0, -1.0]).reshape(1, 1, 2, 1, 1)
    full = (fine, 4, 2, local_rows, 4)
    twist_y = np.stack(
        (np.broadcast_to(cosine, full).reshape(fine, 512), np.broadcast_to(sine * signs, full).reshape(fine, 512)), 0
    )
    angle = two_pi * np.outer(np.arange(kept_y), np.arange(fine)) / fine
    left_y = np.concatenate((np.cos(angle), np.sin(angle)), 0)
    left_y_back = left_y.T
    angle = two_pi * np.outer(np.arange(fine), np.arange(fine)) / fine
    left_x = np.concatenate((np.cos(angle), np.sin(angle)), 0)
    angle = two_pi * np.outer(np.arange(fine), np.arange(local_rows)) / side
    full = (fine, 2, local_rows, 4)
    signs = np.array([1.0, -1.0]).reshape(1, 2, 1, 1)
    twist_x = np.stack(
        (
            np.broadcast_to(np.cos(angle)[:, None, :, None], full).reshape(fine, 128),
            np.broadcast_to(np.sin(angle)[:, None, :, None] * signs, full).reshape(fine, 128),
        ),
        0,
    )
    angle = two_pi * np.outer(np.arange(local_rows), kept_a) / radix
    cosine, sine = (np.cos(angle), np.sin(angle))
    eye_q = np.eye(4)
    forward = np.array([[cosine, -sine], [sine, cosine]])
    right_x = np.einsum("cdja,qp->cjqdap", forward, eye_q).reshape(128, 64)
    turned = np.array([[-sine, cosine], [-cosine, -sine]])
    right_x_back = right_x.T
    right_x_turn = np.einsum("cdja,qp->caqdjp", turned, eye_q).reshape(64, 128)
    return dict(
        right_y=split_table(right_y),
        right_y_back=split_table(right_y.T),
        left_y=split_table(left_y),
        left_y_back=split_table(left_y_back),
        twist_y=twist_y.astype(np.float32),
        left_x=split_table(left_x),
        right_x=split_table(right_x),
        right_x_back=split_table(right_x_back),
        right_x_turn=split_table(right_x_turn),
        twist_x=twist_x.astype(np.float32),
    )


y_in = ("right_y", "twist_y", "left_y")
y_out = ("left_y_back", "twist_y", "right_y_back")
y_both = ("left_y_back", "twist_y", "right_y_back", "right_y", "left_y")
x_in = ("left_x", "twist_x", "right_x")
x_out = ("right_x_back", "right_x_turn", "twist_x", "left_x")
x_both = ("left_x", "twist_x", "right_x", "right_x_back")
x_turn = ("left_x", "twist_x", "right_x", "right_x_turn")
x_all = ("left_x", "twist_x", "right_x", "right_x_back", "right_x_turn")


def parted(values):
    high = values.astype(jnp.bfloat16)
    return (high, (values - high.astype(jnp.float32)).astype(jnp.bfloat16))


def product(first, second):
    return jnp.dot(first, second, preferred_element_type=jnp.float32)


def left_times(table_ref, values):
    high, low = parted(values)
    return product(table_ref[0], high) + (product(table_ref[1], high) + product(table_ref[0], low))


def times_right(values, table_ref):
    high, low = parted(values)
    return product(high, table_ref[0]) + (product(low, table_ref[0]) + product(high, table_ref[1]))


def swapped(values):
    pieces = [
        pltpu.roll(values[:, start : start + 128], 64, 1) for start in range(0, values.shape[1], 128)
    ]
    return pieces[0] if len(pieces) == 1 else jnp.concatenate(pieces, 1)


def half_signs(shape):
    lane = lax.broadcasted_iota(jnp.int32, shape, 1)
    return jnp.where(lane % 128 < 64, 1.0, -1.0).astype(jnp.float32)


def y_forward(tab, field, message_ref, slot, count):
    values = times_right(field, tab["right_y"])
    values = values * tab["twist_y"][0] + swapped(values) * tab["twist_y"][1]
    both = left_times(tab["left_y"], values)
    turned = swapped(both[kept_y:])
    values = both[:kept_y] + turned * half_signs(turned.shape)
    for part in range(4):
        message_ref[pl.ds(part * count + slot, kept_y, stride=4 * count), :] = values[
            :, part * 128 : part * 128 + 128
        ]


def y_inverse(tab, arrived_ref, slot, count):
    values = jnp.concatenate(
        [arrived_ref[pl.ds(part * count + slot, kept_y, stride=4 * count), :] for part in range(4)], 1
    )
    turned = swapped(values)
    stacked = jnp.concatenate((values, turned * -half_signs(turned.shape)), 0)
    values = left_times(tab["left_y_back"], stacked)
    values = values * tab["twist_y"][0] - swapped(values) * tab["twist_y"][1]
    return times_right(values, tab["right_y_back"])


def x_forward(tab, arrived_ref, slot, count):
    values = arrived_ref[pl.ds(slot, fine, stride=count), :] if count > 1 else arrived_ref[...]
    both = left_times(tab["left_x"], values)
    turned = swapped(both[fine:])
    values = both[:fine] + turned * half_signs(turned.shape)
    values = values * tab["twist_x"][0] + swapped(values) * tab["twist_x"][1]
    return times_right(values, tab["right_x"])


def x_inverse(tab, straight, turned_part, message_ref, slot, count):
    if straight is None:
        values = times_right(turned_part, tab["right_x_turn"])
    else:
        values = times_right(straight, tab["right_x_back"])
        if turned_part is not None:
            values = values + times_right(turned_part, tab["right_x_turn"])
    values = values * tab["twist_x"][0] - swapped(values) * tab["twist_x"][1]
    both = left_times(tab["left_x"], values)
    turned = swapped(both[fine:])
    values = both[:fine] - turned * half_signs(turned.shape)
    put(message_ref, values, slot, count)


def put(message_ref, values, slot, count):
    if count > 1:
        message_ref[pl.ds(slot, fine, stride=count), :] = values
    else:
        message_ref[...] = values


def message(count):
    return jax.ShapeDtypeStruct((devices * count, 128), jnp.float32)


field_shape = jax.ShapeDtypeStruct((256, 256), jnp.float32)
spectrum_shape = jax.ShapeDtypeStruct((fine, 64), jnp.float32)


class Fetched:
    def __init__(self, source, target, semaphore):
        self.target = target
        self.copy = pltpu.make_async_copy(source, target, semaphore)
        self.copy.start()
        self.pending = True

    def arrive(self):
        if self.pending:
            self.copy.wait()
            self.pending = False

    def __getitem__(self, index):
        self.arrive()
        return self.target[index]


def run(body, names, inputs, outputs, flops):
    operands = [inputs[0]] + [jnp.asarray(tables()[name]) for name in names] + list(inputs[1:])
    total_in = len(operands)
    total = total_in + len(outputs)

    def kernel(*refs):
        semaphores = refs[-1]
        held = refs[total:-1]
        fetched = [Fetched(refs[i], held[i], semaphores.at[i]) for i in range(total_in)]
        tab = dict(zip(names, fetched[1 : 1 + len(names)]))
        ins = fetched[:1] + fetched[1 + len(names) :]
        outs = held[total_in:]
        sends = {}

        def emit(place):
            copy = pltpu.make_async_copy(
                outs[place], refs[total_in + place], semaphores.at[total_in + place]
            )
            copy.start()
            sends[place] = copy

        body(tab, ins, outs, emit)
        for place in range(len(outs)):
            if place not in sends:
                emit(place)
        for item in fetched:
            item.arrive()
        for copy in sends.values():
            copy.wait()

    outside = pl.BlockSpec(memory_space=pltpu.HBM)
    moved = sum(4 * int(np.prod(a.shape)) for a in list(operands) + list(outputs))
    return pl.pallas_call(
        kernel,
        out_shape=list(outputs),
        in_specs=[outside] * total_in,
        out_specs=[outside] * len(outputs),
        scratch_shapes=[pltpu.VMEM(a.shape, a.dtype) for a in list(operands) + list(outputs)]
        + [pltpu.SemaphoreType.DMA((total,))],
        compiler_params=pltpu.CompilerParams(vmem_limit_bytes=60_000_000),
        cost_estimate=pl.CostEstimate(flops=int(flops * 6e8), bytes_accessed=int(moved), transcendentals=0),
    )(*operands)


def exchange(values):
    count = values.shape[0] // devices
    values = values.reshape(devices, count, 128)
    values = lax.all_to_all(values, mesh_axes, split_axis=0, concat_axis=0, tiled=True)
    return values.reshape(devices * count, 128)


def gather_rows(block):
    pieces = [block[:, start : start + 256] for start in range(0, side, 256)]
    return jnp.concatenate(pieces, 0).T


def scatter_rows(out_ref, field, extra_ref):
    turned = field.T
    for part in range(radix):
        columns = pl.ds(part * 256, 256)
        out_ref[:, columns] = turned[part * local_rows : (part + 1) * local_rows, :] + extra_ref[:, columns]


def wave_tables():
    own = lax.axis_index("rows") * lax.axis_size("cols") + lax.axis_index("cols")
    lane = jnp.arange(64, dtype=jnp.int32)
    digit = (lane // 4) % 8
    mode_y = 4 * own + lane % 4
    row = jnp.arange(fine, dtype=jnp.int32)
    mode_x = 256 * jnp.where(digit < 4, digit, digit - 8)[None, :] + row[:, None]
    wave_x = (2.0 * jnp.pi / side) * mode_x.astype(jnp.float32)
    wave_y = jnp.broadcast_to(((2.0 * jnp.pi / side) * mode_y.astype(jnp.float32))[None, :], wave_x.shape)
    weight = jnp.where(mode_y == 0, 1.0, 2.0)[None, :] / (side * side)
    keep = jnp.where(jnp.abs(mode_x) < side // 4, weight, 0.0).astype(jnp.float32)
    magnitude = jnp.sqrt(wave_x * wave_x + wave_y * wave_y)
    return jnp.stack((keep, magnitude, wave_x, wave_y), 0)


def per_device(elevation, potential, elevation_cot, potential_cot):
    waves = wave_tables()

    def start(tab, ins, outs, emit):
        surface = gather_rows(ins[0][...])
        outs[0][...] = surface
        emit(0)
        y_forward(tab, gather_rows(ins[1][...]), outs[1], 1, 2)
        y_forward(tab, surface, outs[1], 0, 2)

    elev, sent = run(start, y_in, (elevation, potential), (field_shape, message(2)), 2)
    first = exchange(sent)

    def cotangents(tab, ins, outs, emit):
        outs[0][...] = section_step * gather_rows(ins[0][...])
        rate = section_step * gather_rows(ins[1][...])
        outs[1][...] = rate
        y_forward(tab, -stiffness * rate, outs[2], 0, 1)

    rate_elev, rate_pot, bend_sent = run(
        cotangents, y_in, (elevation_cot, potential_cot), (field_shape, field_shape, message(1)), 1
    )

    def second(tab, ins, outs, emit):
        spec = x_forward(tab, ins[0], 1, 2)
        outs[1][...] = spec * ins[1][0]
        spec = spec * ins[1][0]
        for degree in range(4):
            spec = spec * ins[1][1]
            x_inverse(tab, spec, None, outs[0], degree, 4)

    sent, pot_spec = run(second, x_both, (first, waves), (message(4), spectrum_shape), 2)
    lifts = exchange(sent)

    def slopes(tab, ins, outs, emit):
        spec = x_forward(tab, ins[0], 0, 2) * ins[2][0]
        x_inverse(tab, None, spec * ins[2][2], outs[0], 0, 1)
        x_inverse(tab, None, spec * ins[2][3], outs[1], 0, 1)
        spec = ins[1][...]
        x_inverse(tab, None, spec * ins[2][2], outs[2], 0, 1)
        x_inverse(tab, None, spec * ins[2][3], outs[3], 0, 1)

    slope_x_sent, slope_y_sent, flow_x_sent, flow_y_sent = run(
        slopes, x_turn, (first, pot_spec, waves), (message(1),) * 4, 2
    )

    def third(tab, ins, outs, emit):
        lifted = y_inverse(tab, ins[0], 0, 4)
        outs[1][...] = lifted
        emit(1)
        y_forward(tab, -ins[1][...] * lifted, outs[0], 0, 2)
        put(outs[0], ins[2][...], 1, 2)

    sent, lift_11 = run(third, y_both, (lifts, elev, bend_sent), (message(2), field_shape), 2)
    arrived = exchange(sent)

    def inverse_of(slots, count):
        def body(tab, ins, outs, emit):
            for place, slot in enumerate(slots):
                outs[place][...] = y_inverse(tab, ins[0], slot, count)
                emit(place)

        return body

    lift_12, lift_13, lift_14 = run(inverse_of((1, 2, 3), 4), y_out, (lifts,), (field_shape,) * 3, 3)

    def fourth(tab, ins, outs, emit):
        spec = x_forward(tab, ins[0], 0, 2) * ins[1][0]
        for degree in range(3):
            spec = spec * ins[1][1]
            x_inverse(tab, spec, None, outs[0], degree, 4)
        put(outs[0], ins[2][...], 3, 4)

    (sent,) = run(fourth, x_both, (arrived, waves, slope_x_sent), (message(4),), 2)

    def spectra_of(slots, count):
        def body(tab, ins, outs, emit):
            for place, slot in enumerate(slots):
                outs[place][...] = x_forward(tab, ins[0], slot, count) * ins[1][0]

        return body

    (bend_spec,) = run(spectra_of((1,), 2), x_in, (arrived, waves), (spectrum_shape,), 1)
    arrived = exchange(sent)

    def fifth(tab, ins, outs, emit):
        lifted = y_inverse(tab, ins[0], 0, 4)
        outs[1][...] = lifted
        emit(1)
        surface = ins[1][...]
        y_forward(tab, -surface * lifted - (surface * surface / 2.0) * ins[2][...], outs[0], 0, 1)

    sent, lift_21 = run(fifth, y_both, (arrived, elev, lift_12), (message(1), field_shape), 2)
    lift_22, lift_23, slope_x = run(inverse_of((1, 2, 3), 4), y_out, (arrived,), (field_shape,) * 3, 3)
    arrived = exchange(sent)

    def sixth(tab, ins, outs, emit):
        spec = x_forward(tab, ins[0], 0, 1) * ins[1][0]
        for degree in range(2):
            spec = spec * ins[1][1]
            x_inverse(tab, spec, None, outs[0], degree, 4)
        put(outs[0], ins[2][...], 2, 4)
        put(outs[0], ins[3][...], 3, 4)

    (sent,) = run(sixth, x_both, (arrived, waves, slope_y_sent, flow_x_sent), (message(4),), 2)
    arrived = exchange(sent)

    def seventh(tab, ins, outs, emit):
        lifted = y_inverse(tab, ins[0], 0, 4)
        outs[1][...] = lifted
        emit(1)
        surface = ins[1][...]
        square = surface * surface / 2.0
        cube = square * surface / 3.0
        y_forward(tab, -surface * lifted - square * ins[2][...] - cube * ins[3][...], outs[0], 0, 1)

    sent, lift_31 = run(seventh, y_both, (arrived, elev, lift_22, lift_13), (message(1), field_shape), 2)
    lift_32, slope_y, flow_x = run(inverse_of((1, 2, 3), 4), y_out, (arrived,), (field_shape,) * 3, 3)
    arrived = exchange(sent)

    def eighth(tab, ins, outs, emit):
        spec = x_forward(tab, ins[0], 0, 1) * (ins[1][0] * ins[1][1])
        x_inverse(tab, spec, None, outs[0], 0, 2)
        put(outs[0], ins[2][...], 1, 2)

    (sent,) = run(eighth, x_both, (arrived, waves, flow_y_sent), (message(2),), 1)
    arrived = exchange(sent)

    square = elev * elev / 2.0
    cube = square * elev / 3.0
    partial = (
        lift_11
        + lift_21
        + lift_31
        + elev * (lift_12 + lift_22 + lift_32)
        + square * (lift_13 + lift_23)
        + cube * lift_14
    )
    growth = lift_12 + lift_22 + lift_32 + elev * (lift_13 + lift_23) + square * lift_14
    steepness = 1.0 + slope_x * slope_x + slope_y * slope_y

    def ninth(tab, ins, outs, emit):
        vertical = ins[1][...] + y_inverse(tab, ins[0], 0, 2)
        vertical_cot = ins[2][...] * (ins[3][...] + vertical * ins[4][...])
        outs[1][...] = vertical
        emit(1)
        outs[2][...] = vertical_cot
        emit(2)
        y_forward(tab, vertical_cot, outs[0], 0, 2)
        y_forward(tab, ins[5][...] * vertical_cot, outs[0], 1, 2)

    sent, vertical, vertical_cot = run(
        ninth,
        y_both,
        (arrived, partial, steepness, rate_elev, rate_pot, elev),
        (message(2), field_shape, field_shape),
        3,
    )
    (flow_y,) = run(inverse_of((1,), 2), y_out, (arrived,), (field_shape,), 1)
    arrived = exchange(sent)
    steep_cot = vertical * rate_elev + 0.5 * vertical * vertical * rate_pot

    def forward_all(tab, ins, outs, emit):
        for place in range(len(ins)):
            y_forward(tab, ins[place][...], outs[place], 0, 1)
            emit(place)

    def sends_of(*fields):
        return run(forward_all, y_in, fields, (message(1),) * len(fields), len(fields))

    square_cot_sent, cube_cot_sent = sends_of(square * vertical_cot, cube * vertical_cot)
    slope_x_cot, slope_y_cot = sends_of(
        -flow_x * rate_elev + 2.0 * slope_x * steep_cot, -flow_y * rate_elev + 2.0 * slope_y * steep_cot
    )
    flow_x_cot, flow_y_cot = sends_of(
        -slope_x * rate_elev - flow_x * rate_pot, -slope_y * rate_elev - flow_y * rate_pot
    )

    def tenth(tab, ins, outs, emit):
        spec = x_forward(tab, ins[0], 0, 2) * ins[1][0]
        outs[1][...] = spec
        emit(1)
        x_inverse(tab, spec * ins[1][1], None, outs[0], 0, 1)

    sent, cot_spec = run(tenth, x_both, (arrived, waves), (message(1), spectrum_shape), 1)
    (elev_cot_spec,) = run(spectra_of((1,), 2), x_in, (arrived, waves), (spectrum_shape,), 1)
    arrived = exchange(sent)

    def eleventh(tab, ins, outs, emit):
        lifted = y_inverse(tab, ins[0], 0, 1)
        outs[1][...] = lifted
        emit(1)
        surface = ins[1][...]
        y_forward(tab, surface * lifted, outs[0], 0, 4)
        y_forward(tab, (surface * surface / 2.0) * lifted, outs[0], 1, 4)
        put(outs[0], ins[2][...], 2, 4)
        put(outs[0], ins[3][...], 3, 4)

    sent, fourth_cot = run(
        eleventh, y_both, (arrived, elev, square_cot_sent, cube_cot_sent), (message(4), field_shape), 3
    )
    (cube_fourth_sent,) = sends_of(cube * fourth_cot)
    arrived = exchange(sent)

    def twelfth(tab, ins, outs, emit):
        spec = x_forward(tab, ins[0], 0, 4) * ins[1][0]
        spec = ins[1][1] * ((ins[2][...] - spec) + ins[1][1] * ins[3][...])
        x_inverse(tab, spec, None, outs[0], 0, 1)

    (sent,) = run(twelfth, x_both, (arrived, waves, cot_spec, elev_cot_spec), (message(1),), 1)
    square_fourth_spec, square_cot_spec, cube_cot_spec = run(
        spectra_of((1, 2, 3), 4), x_in, (arrived, waves), (spectrum_shape,) * 3, 1
    )
    arrived = exchange(sent)

    def thirteenth(tab, ins, outs, emit):
        lifted = y_inverse(tab, ins[0], 0, 1)
        outs[1][...] = lifted
        emit(1)
        y_forward(tab, ins[1][...] * lifted, outs[0], 0, 4)
        for slot in range(1, 4):
            put(outs[0], ins[1 + slot][...], slot, 4)

    sent, third_cot = run(
        thirteenth,
        y_both,
        (arrived, elev, cube_fourth_sent, slope_x_cot, slope_y_cot),
        (message(4), field_shape),
        2,
    )
    (square_third_sent,) = sends_of(square * third_cot)
    arrived = exchange(sent)

    def fourteenth(tab, ins, outs, emit):
        wave = ins[1][1]
        spec = x_forward(tab, ins[0], 0, 4) * ins[1][0]
        spec = wave * (
            (ins[2][...] - spec) + wave * ((ins[3][...] - ins[4][...]) + wave * ins[5][...])
        )
        x_inverse(tab, spec, None, outs[0], 0, 1)

    (sent,) = run(
        fourteenth,
        x_both,
        (arrived, waves, cot_spec, elev_cot_spec, square_fourth_spec, square_cot_spec),
        (message(1),),
        1,
    )

    def gathered(tab, ins, outs, emit):
        wave = ins[1][1]
        cube_fourth = x_forward(tab, ins[0], 1, 4) * ins[1][0]
        outs[0][...] = wave * (
            ins[2][...]
            + wave * (ins[3][...] + wave * ((ins[4][...] - cube_fourth) + wave * ins[5][...]))
        )
        slope_x_spec = x_forward(tab, ins[0], 2, 4) * ins[1][0]
        slope_y_spec = x_forward(tab, ins[0], 3, 4) * ins[1][0]
        outs[1][...] = -(ins[1][2] * slope_x_spec + ins[1][3] * slope_y_spec)
        outs[2][...] = ins[6][...] * (wave * wave) * (wave * wave)

    pot_part, elev_turn, elev_part = run(
        gathered,
        x_in,
        (arrived, waves, cot_spec, elev_cot_spec, square_cot_spec, cube_cot_spec, bend_spec),
        (spectrum_shape,) * 3,
        1,
    )
    arrived = exchange(sent)

    def fifteenth(tab, ins, outs, emit):
        lifted = y_inverse(tab, ins[0], 0, 1)
        outs[1][...] = lifted
        emit(1)
        y_forward(tab, ins[1][...] * lifted, outs[0], 0, 4)
        for slot in range(1, 4):
            put(outs[0], ins[1 + slot][...], slot, 4)

    sent, second_cot = run(
        fifteenth,
        y_both,
        (arrived, elev, square_third_sent, flow_x_cot, flow_y_cot),
        (message(4), field_shape),
        2,
    )
    arrived = exchange(sent)

    def elevation_side(tab, ins, outs, emit):
        x_inverse(tab, ins[0][...], ins[1][...], outs[0], 0, 1)

    (elev_sent,) = run(elevation_side, x_out, (elev_part, elev_turn), (message(1),), 1)

    def sixteenth(tab, ins, outs, emit):
        wave = ins[1][1]
        keep = ins[1][0]
        first_part = x_forward(tab, ins[0], 0, 4) * keep
        second_part = x_forward(tab, ins[0], 1, 4) * keep
        flow_part = x_forward(tab, ins[0], 2, 4) * ins[1][2] + x_forward(tab, ins[0], 3, 4) * ins[1][3]
        straight = ins[2][...] - wave * (first_part + wave * second_part)
        x_inverse(tab, straight, -flow_part * keep, outs[0], 1, 2)
        put(outs[0], ins[3][...], 0, 2)

    (sent,) = run(sixteenth, x_all, (arrived, waves, pot_part, elev_sent), (message(2),), 2)
    arrived = exchange(sent)

    grad = (
        vertical_cot * growth
        - (lift_31 + elev * lift_22 + square * lift_13) * fourth_cot
        - (lift_21 + elev * lift_12) * third_cot
        - lift_11 * second_cot
        - rate_pot
    )

    def finish(tab, ins, outs, emit):
        scatter_rows(outs[1], y_inverse(tab, ins[0], 1, 2), ins[3])
        emit(1)
        scatter_rows(outs[0], ins[1][...] + y_inverse(tab, ins[0], 0, 2), ins[2])

    block = jax.ShapeDtypeStruct(elevation.shape, jnp.float32)
    elevation_grad, potential_grad = run(
        finish, y_out, (arrived, grad, elevation_cot, potential_cot), (block, block), 2
    )
    return (elevation_grad, potential_grad)


def solution(mesh):
    spec = P(mesh_axes, None)
    return jax.shard_map(
        per_device, mesh=mesh, in_specs=(spec,) * 4, out_specs=(spec, spec), check_vma=False
    )
```

```python
import functools

import jax
import jax.numpy as jnp
import numpy as np
from jax import lax
from jax.experimental import pallas as pl
from jax.experimental.pallas import tpu as pltpu
from jax.sharding import PartitionSpec as P

stiffness = 0.05
section_step = 0.25
side = 4096
devices = 256
local_rows = 16
radix = 16
fine = 256
kept_y = 64
kept_a = np.array([0, 1, 2, 3, 12, 13, 14, 15])
mesh_axes = ("rows", "cols")


def split_table(table):
    table = table.astype(np.float32)
    high = table.astype(jnp.bfloat16)
    low = (table - high.astype(np.float32)).astype(jnp.bfloat16)
    return np.stack((high, low), 0)


@functools.lru_cache(maxsize=None)
def tables():
    two_pi = 2.0 * np.pi
    eye_j = np.eye(local_rows)
    residue = np.arange(radix)
    angle = two_pi * np.outer(np.arange(radix), residue) / radix
    parts = np.stack((np.cos(angle), -np.sin(angle)), 0).reshape(2, radix, 4, 4)
    right_y = np.einsum("cthl,jk->tjhckl", parts, eye_j).reshape(radix * local_rows, 512)
    angle = two_pi * np.outer(np.arange(fine), residue) / side
    cosine = np.cos(angle).reshape(fine, 4, 1, 1, 4)
    sine = np.sin(angle).reshape(fine, 4, 1, 1, 4)
    signs = np.array([1.0, -1.0]).reshape(1, 1, 2, 1, 1)
    full = (fine, 4, 2, local_rows, 4)
    twist_y = np.stack(
        (np.broadcast_to(cosine, full).reshape(fine, 512), np.broadcast_to(sine * signs, full).reshape(fine, 512)), 0
    )
    angle = two_pi * np.outer(np.arange(kept_y), np.arange(fine)) / fine
    left_y = np.concatenate((np.cos(angle), np.sin(angle)), 0)
    left_y_back = left_y.T
    angle = two_pi * np.outer(np.arange(fine), np.arange(fine)) / fine
    left_x = np.concatenate((np.cos(angle), np.sin(angle)), 0)
    angle = two_pi * np.outer(np.arange(fine), np.arange(local_rows)) / side
    full = (fine, 2, local_rows, 4)
    signs = np.array([1.0, -1.0]).reshape(1, 2, 1, 1)
    twist_x = np.stack(
        (
            np.broadcast_to(np.cos(angle)[:, None, :, None], full).reshape(fine, 128),
            np.broadcast_to(np.sin(angle)[:, None, :, None] * signs, full).reshape(fine, 128),
        ),
        0,
    )
    angle = two_pi * np.outer(np.arange(local_rows), kept_a) / radix
    cosine, sine = (np.cos(angle), np.sin(angle))
    eye_q = np.eye(4)
    forward = np.array([[cosine, -sine], [sine, cosine]])
    right_x = np.einsum("cdja,qp->cjqdap", forward, eye_q).reshape(128, 64)
    turned = np.array([[-sine, cosine], [-cosine, -sine]])
    right_x_back = right_x.T
    right_x_turn = np.einsum("cdja,qp->caqdjp", turned, eye_q).reshape(64, 128)
    return dict(
        right_y=split_table(right_y),
        right_y_back=split_table(right_y.T),
        left_y=split_table(left_y),
        left_y_back=split_table(left_y_back),
        twist_y=twist_y.astype(np.float32),
        left_x=split_table(left_x),
        right_x=split_table(right_x),
        right_x_back=split_table(right_x_back),
        right_x_turn=split_table(right_x_turn),
        twist_x=twist_x.astype(np.float32),
    )


y_in = ("right_y", "twist_y", "left_y")
y_out = ("left_y_back", "twist_y", "right_y_back")
y_both = ("left_y_back", "twist_y", "right_y_back", "right_y", "left_y")
x_in = ("left_x", "twist_x", "right_x")
x_out = ("right_x_back", "right_x_turn", "twist_x", "left_x")
x_both = ("left_x", "twist_x", "right_x", "right_x_back")
x_turn = ("left_x", "twist_x", "right_x", "right_x_turn")
x_all = ("left_x", "twist_x", "right_x", "right_x_back", "right_x_turn")


def parted(values):
    high = values.astype(jnp.bfloat16)
    return (high, (values - high.astype(jnp.float32)).astype(jnp.bfloat16))


def product(first, second):
    return jnp.dot(first, second, preferred_element_type=jnp.float32)


def left_times(table_ref, values):
    high, low = parted(values)
    return product(table_ref[0], high) + (product(table_ref[1], high) + product(table_ref[0], low))


def times_right(values, table_ref):
    high, low = parted(values)
    return product(high, table_ref[0]) + (product(low, table_ref[0]) + product(high, table_ref[1]))


def swapped(values):
    pieces = [
        pltpu.roll(values[:, start : start + 128], 64, 1) for start in range(0, values.shape[1], 128)
    ]
    return pieces[0] if len(pieces) == 1 else jnp.concatenate(pieces, 1)


def half_signs(shape):
    lane = lax.broadcasted_iota(jnp.int32, shape, 1)
    return jnp.where(lane % 128 < 64, 1.0, -1.0).astype(jnp.float32)


def y_forward(tab, field, message_ref, slot, count):
    values = times_right(field, tab["right_y"])
    values = values * tab["twist_y"][0] + swapped(values) * tab["twist_y"][1]
    both = left_times(tab["left_y"], values)
    turned = swapped(both[kept_y:])
    values = both[:kept_y] + turned * half_signs(turned.shape)
    for part in range(4):
        message_ref[pl.ds(part * count + slot, kept_y, stride=4 * count), :] = values[
            :, part * 128 : part * 128 + 128
        ]


def y_inverse(tab, arrived_ref, slot, count):
    values = jnp.concatenate(
        [arrived_ref[pl.ds(part * count + slot, kept_y, stride=4 * count), :] for part in range(4)], 1
    )
    turned = swapped(values)
    stacked = jnp.concatenate((values, turned * -half_signs(turned.shape)), 0)
    values = left_times(tab["left_y_back"], stacked)
    values = values * tab["twist_y"][0] - swapped(values) * tab["twist_y"][1]
    return times_right(values, tab["right_y_back"])


def x_forward(tab, arrived_ref, slot, count):
    values = arrived_ref[pl.ds(slot, fine, stride=count), :] if count > 1 else arrived_ref[...]
    both = left_times(tab["left_x"], values)
    turned = swapped(both[fine:])
    values = both[:fine] + turned * half_signs(turned.shape)
    values = values * tab["twist_x"][0] + swapped(values) * tab["twist_x"][1]
    return times_right(values, tab["right_x"])


def x_inverse(tab, straight, turned_part, message_ref, slot, count):
    if straight is None:
        values = times_right(turned_part, tab["right_x_turn"])
    else:
        values = times_right(straight, tab["right_x_back"])
        if turned_part is not None:
            values = values + times_right(turned_part, tab["right_x_turn"])
    values = values * tab["twist_x"][0] - swapped(values) * tab["twist_x"][1]
    both = left_times(tab["left_x"], values)
    turned = swapped(both[fine:])
    values = both[:fine] - turned * half_signs(turned.shape)
    put(message_ref, values, slot, count)


def put(message_ref, values, slot, count):
    if count > 1:
        message_ref[pl.ds(slot, fine, stride=count), :] = values
    else:
        message_ref[...] = values


def message(count):
    return pltpu.HBM((devices * count, 128), jnp.float32)


part_shape = pltpu.HBM((devices, 128), jnp.float32)
field_shape = pltpu.HBM((256, 256), jnp.float32)
spectrum_shape = pltpu.HBM((fine, 64), jnp.float32)


class Fetched:
    def __init__(self, source, target, semaphore):
        self.target = target
        self.copy = pltpu.make_async_copy(source, target, semaphore)
        self.copy.start()
        self.pending = True

    def arrive(self):
        if self.pending:
            self.copy.wait()
            self.pending = False

    def __getitem__(self, index):
        self.arrive()
        return self.target[index]


def is_near(shape):
    return shape.memory_space == pltpu.VMEM


resident_names = ("left_x", "twist_x", "right_x", "right_x_back", "twist_y", "left_y_back")


def stage_tables():
    names = resident_names
    values = [pltpu.with_memory_space_constraint(jnp.asarray(tables()[name]), pltpu.HBM) for name in names]
    count = len(values)

    def kernel(*refs):
        copies = [
            pltpu.make_async_copy(refs[i], refs[count + i], refs[-1].at[i]) for i in range(count)
        ]
        for copy in copies:
            copy.start()
        for copy in copies:
            copy.wait()

    staged = pl.pallas_call(
        kernel,
        out_shape=[pltpu.VMEM(a.shape, a.dtype) for a in values],
        in_specs=[pl.BlockSpec(memory_space=pltpu.HBM)] * count,
        out_specs=[pl.BlockSpec(memory_space=pltpu.VMEM)] * count,
        scratch_shapes=[pltpu.SemaphoreType.DMA((count,))],
        compiler_params=pltpu.CompilerParams(vmem_limit_bytes=vmem_limit),
        cost_estimate=pl.CostEstimate(flops=0, bytes_accessed=8_000_000, transcendentals=0),
    )(*values)
    return dict(zip(names, staged))


vmem_limit = 24_000_000


def run(staged, body, names, inputs, outputs, flops):
    staged = staged or {}
    operands = [inputs[0]] + [
        staged[name] if name in staged else jnp.asarray(tables()[name]) for name in names
    ]
    operands = operands + list(inputs[1:])
    near = {1 + place for place, name in enumerate(names) if name in staged}
    near = near | ({0} if inputs[0].shape[1] == 128 else set())
    far = set(range(len(operands))) - near
    operands = [
        pltpu.with_memory_space_constraint(a, pltpu.HBM if place in far else pltpu.VMEM)
        for place, a in enumerate(operands)
    ]
    total_in = len(operands)
    total = total_in + len(outputs)
    moving = sorted(far)
    leaving = [place for place, shape in enumerate(outputs) if not is_near(shape)]

    def kernel(*refs):
        semaphores = refs[-1]
        held = refs[total:-1]
        fetched = list(refs[:total_in])
        for slot, place in enumerate(moving):
            fetched[place] = Fetched(refs[place], held[slot], semaphores.at[place])
        tab = dict(zip(names, fetched[1 : 1 + len(names)]))
        ins = fetched[:1] + fetched[1 + len(names) :]
        outs = list(refs[total_in:total])
        for slot, place in enumerate(leaving):
            outs[place] = held[len(moving) + slot]
        sends = {}

        def emit(place):
            if place in leaving:
                copy = pltpu.make_async_copy(
                    outs[place], refs[total_in + place], semaphores.at[total_in + place]
                )
                copy.start()
                sends[place] = copy

        body(tab, ins, outs, emit)
        for place in range(len(outs)):
            if place not in sends:
                emit(place)
        for place in moving:
            fetched[place].arrive()
        for copy in sends.values():
            copy.wait()

    outside = pl.BlockSpec(memory_space=pltpu.HBM)
    inside = pl.BlockSpec(memory_space=pltpu.VMEM)
    moved = sum(4 * int(np.prod(a.shape)) for a in list(operands) + list(outputs))
    scratch = [operands[place] for place in moving] + [outputs[place] for place in leaving]
    return pl.pallas_call(
        kernel,
        out_shape=list(outputs),
        in_specs=[outside if place in far else inside for place in range(total_in)],
        out_specs=[inside if is_near(shape) else outside for shape in outputs],
        scratch_shapes=[pltpu.VMEM(a.shape, a.dtype) for a in scratch]
        + [pltpu.SemaphoreType.DMA((total,))],
        compiler_params=pltpu.CompilerParams(vmem_limit_bytes=vmem_limit),
        cost_estimate=pl.CostEstimate(flops=int(flops * 6e8), bytes_accessed=int(moved), transcendentals=0),
    )(*operands)


def exchange(values):
    count = values.shape[0] // devices
    values = values.reshape(devices, count, 128)
    values = lax.all_to_all(values, mesh_axes, split_axis=0, concat_axis=0, tiled=True)
    return values.reshape(devices * count, 128)


def gather_rows(block):
    pieces = [block[:, start : start + 256] for start in range(0, side, 256)]
    return jnp.concatenate(pieces, 0).T


def scatter_rows(out_ref, field, extra_ref):
    turned = field.T
    for part in range(radix):
        columns = pl.ds(part * 256, 256)
        out_ref[:, columns] = turned[part * local_rows : (part + 1) * local_rows, :] + extra_ref[:, columns]


def wave_tables():
    own = lax.axis_index("rows") * lax.axis_size("cols") + lax.axis_index("cols")
    lane = jnp.arange(64, dtype=jnp.int32)
    digit = (lane // 4) % 8
    mode_y = 4 * own + lane % 4
    row = jnp.arange(fine, dtype=jnp.int32)
    mode_x = 256 * jnp.where(digit < 4, digit, digit - 8)[None, :] + row[:, None]
    wave_x = (2.0 * jnp.pi / side) * mode_x.astype(jnp.float32)
    wave_y = jnp.broadcast_to(((2.0 * jnp.pi / side) * mode_y.astype(jnp.float32))[None, :], wave_x.shape)
    weight = jnp.where(mode_y == 0, 1.0, 2.0)[None, :] / (side * side)
    keep = jnp.where(jnp.abs(mode_x) < side // 4, weight, 0.0).astype(jnp.float32)
    magnitude = jnp.sqrt(wave_x * wave_x + wave_y * wave_y)
    return (jnp.stack((keep, magnitude), 0), jnp.stack((wave_x, wave_y), 0))


def per_device(elevation, potential, elevation_cot, potential_cot):
    waves, turns = wave_tables()

    def start(tab, ins, outs, emit):
        surface = gather_rows(ins[0][...])
        outs[0][...] = surface
        emit(0)
        y_forward(tab, gather_rows(ins[1][...]), outs[1], 1, 2)
        y_forward(tab, surface, outs[1], 0, 2)

    elev, sent = run(None, start, y_in, (elevation, potential), (field_shape, message(2)), 2)
    first = exchange(sent)
    staged = stage_tables()

    def cotangents(tab, ins, outs, emit):
        outs[0][...] = section_step * gather_rows(ins[0][...])
        rate = section_step * gather_rows(ins[1][...])
        outs[1][...] = rate
        y_forward(tab, -stiffness * rate, outs[2], 0, 1)

    rate_elev, rate_pot, bend_sent = run(
        staged, cotangents, y_in, (elevation_cot, potential_cot), (field_shape, field_shape, part_shape), 1
    )

    def second(tab, ins, outs, emit):
        spec = x_forward(tab, ins[0], 1, 2)
        outs[1][...] = spec * ins[1][0]
        spec = spec * ins[1][0]
        for degree in range(4):
            spec = spec * ins[1][1]
            x_inverse(tab, spec, None, outs[0], degree, 4)

    sent, pot_spec = run(staged, second, x_both, (first, waves), (message(4), spectrum_shape), 2)
    lifts = exchange(sent)

    def slopes(tab, ins, outs, emit):
        spec = x_forward(tab, ins[0], 0, 2) * ins[2][0]
        x_inverse(tab, None, spec * ins[3][0], outs[0], 0, 1)
        x_inverse(tab, None, spec * ins[3][1], outs[1], 0, 1)
        spec = ins[1][...]
        x_inverse(tab, None, spec * ins[3][0], outs[2], 0, 1)
        x_inverse(tab, None, spec * ins[3][1], outs[3], 0, 1)

    slope_x_sent, slope_y_sent, flow_x_sent, flow_y_sent = run(
        staged, slopes, x_turn, (first, pot_spec, waves, turns), (part_shape,) * 4, 2
    )

    def third(tab, ins, outs, emit):
        lifted = y_inverse(tab, ins[0], 0, 4)
        outs[1][...] = lifted
        emit(1)
        y_forward(tab, -ins[1][...] * lifted, outs[0], 0, 2)
        put(outs[0], ins[2][...], 1, 2)

    sent, lift_11 = run(staged, third, y_both, (lifts, elev, bend_sent), (message(2), field_shape), 2)
    arrived = exchange(sent)

    def inverse_of(slots, count):
        def body(tab, ins, outs, emit):
            for place, slot in enumerate(slots):
                outs[place][...] = y_inverse(tab, ins[0], slot, count)
                emit(place)

        return body

    lift_12, lift_13, lift_14 = run(staged, inverse_of((1, 2, 3), 4), y_out, (lifts,), (field_shape,) * 3, 3)

    def fourth(tab, ins, outs, emit):
        spec = x_forward(tab, ins[0], 0, 2) * ins[1][0]
        for degree in range(3):
            spec = spec * ins[1][1]
            x_inverse(tab, spec, None, outs[0], degree, 4)
        put(outs[0], ins[2][...], 3, 4)

    (sent,) = run(staged, fourth, x_both, (arrived, waves, slope_x_sent), (message(4),), 2)

    def spectra_of(slots, count):
        def body(tab, ins, outs, emit):
            for place, slot in enumerate(slots):
                outs[place][...] = x_forward(tab, ins[0], slot, count) * ins[1][0]

        return body

    (bend_spec,) = run(staged, spectra_of((1,), 2), x_in, (arrived, waves), (spectrum_shape,), 1)
    arrived = exchange(sent)

    def fifth(tab, ins, outs, emit):
        lifted = y_inverse(tab, ins[0], 0, 4)
        outs[1][...] = lifted
        emit(1)
        surface = ins[1][...]
        y_forward(tab, -surface * lifted - (surface * surface / 2.0) * ins[2][...], outs[0], 0, 1)

    sent, lift_21 = run(staged, fifth, y_both, (arrived, elev, lift_12), (message(1), field_shape), 2)
    lift_22, lift_23, slope_x = run(staged, inverse_of((1, 2, 3), 4), y_out, (arrived,), (field_shape,) * 3, 3)
    arrived = exchange(sent)

    def sixth(tab, ins, outs, emit):
        spec = x_forward(tab, ins[0], 0, 1) * ins[1][0]
        for degree in range(2):
            spec = spec * ins[1][1]
            x_inverse(tab, spec, None, outs[0], degree, 4)
        put(outs[0], ins[2][...], 2, 4)
        put(outs[0], ins[3][...], 3, 4)

    (sent,) = run(staged, sixth, x_both, (arrived, waves, slope_y_sent, flow_x_sent), (message(4),), 2)
    arrived = exchange(sent)

    def seventh(tab, ins, outs, emit):
        lifted = y_inverse(tab, ins[0], 0, 4)
        outs[1][...] = lifted
        emit(1)
        surface = ins[1][...]
        square = surface * surface / 2.0
        cube = square * surface / 3.0
        y_forward(tab, -surface * lifted - square * ins[2][...] - cube * ins[3][...], outs[0], 0, 1)

    sent, lift_31 = run(staged, seventh, y_both, (arrived, elev, lift_22, lift_13), (message(1), field_shape), 2)
    lift_32, slope_y, flow_x = run(staged, inverse_of((1, 2, 3), 4), y_out, (arrived,), (field_shape,) * 3, 3)
    arrived = exchange(sent)

    def eighth(tab, ins, outs, emit):
        spec = x_forward(tab, ins[0], 0, 1) * (ins[1][0] * ins[1][1])
        x_inverse(tab, spec, None, outs[0], 0, 2)
        put(outs[0], ins[2][...], 1, 2)

    (sent,) = run(staged, eighth, x_both, (arrived, waves, flow_y_sent), (message(2),), 1)
    arrived = exchange(sent)

    square = elev * elev / 2.0
    cube = square * elev / 3.0
    partial = (
        lift_11
        + lift_21
        + lift_31
        + elev * (lift_12 + lift_22 + lift_32)
        + square * (lift_13 + lift_23)
        + cube * lift_14
    )
    growth = lift_12 + lift_22 + lift_32 + elev * (lift_13 + lift_23) + square * lift_14
    steepness = 1.0 + slope_x * slope_x + slope_y * slope_y

    def ninth(tab, ins, outs, emit):
        vertical = ins[1][...] + y_inverse(tab, ins[0], 0, 2)
        vertical_cot = ins[2][...] * (ins[3][...] + vertical * ins[4][...])
        outs[1][...] = vertical
        emit(1)
        outs[2][...] = vertical_cot
        emit(2)
        y_forward(tab, vertical_cot, outs[0], 0, 2)
        y_forward(tab, ins[5][...] * vertical_cot, outs[0], 1, 2)

    sent, vertical, vertical_cot = run(
        staged, ninth,
        y_both,
        (arrived, partial, steepness, rate_elev, rate_pot, elev),
        (message(2), field_shape, field_shape),
        3,
    )
    (flow_y,) = run(staged, inverse_of((1,), 2), y_out, (arrived,), (field_shape,), 1)
    arrived = exchange(sent)
    steep_cot = vertical * rate_elev + 0.5 * vertical * vertical * rate_pot

    def forward_all(tab, ins, outs, emit):
        for place in range(len(ins)):
            y_forward(tab, ins[place][...], outs[place], 0, 1)
            emit(place)

    def sends_of(*fields):
        return run(staged, forward_all, y_in, fields, (part_shape,) * len(fields), len(fields))

    square_cot_sent, cube_cot_sent = sends_of(square * vertical_cot, cube * vertical_cot)
    slope_x_cot, slope_y_cot = sends_of(
        -flow_x * rate_elev + 2.0 * slope_x * steep_cot, -flow_y * rate_elev + 2.0 * slope_y * steep_cot
    )
    flow_x_cot, flow_y_cot = sends_of(
        -slope_x * rate_elev - flow_x * rate_pot, -slope_y * rate_elev - flow_y * rate_pot
    )

    def tenth(tab, ins, outs, emit):
        spec = x_forward(tab, ins[0], 0, 2) * ins[1][0]
        outs[1][...] = spec
        emit(1)
        x_inverse(tab, spec * ins[1][1], None, outs[0], 0, 1)

    sent, cot_spec = run(staged, tenth, x_both, (arrived, waves), (message(1), spectrum_shape), 1)
    (elev_cot_spec,) = run(staged, spectra_of((1,), 2), x_in, (arrived, waves), (spectrum_shape,), 1)
    arrived = exchange(sent)

    def eleventh(tab, ins, outs, emit):
        lifted = y_inverse(tab, ins[0], 0, 1)
        outs[1][...] = lifted
        emit(1)
        surface = ins[1][...]
        y_forward(tab, surface * lifted, outs[0], 0, 4)
        y_forward(tab, (surface * surface / 2.0) * lifted, outs[0], 1, 4)
        put(outs[0], ins[2][...], 2, 4)
        put(outs[0], ins[3][...], 3, 4)

    sent, fourth_cot = run(
        staged, eleventh, y_both, (arrived, elev, square_cot_sent, cube_cot_sent), (message(4), field_shape), 3
    )
    (cube_fourth_sent,) = sends_of(cube * fourth_cot)
    arrived = exchange(sent)

    def twelfth(tab, ins, outs, emit):
        spec = x_forward(tab, ins[0], 0, 4) * ins[1][0]
        spec = ins[1][1] * ((ins[2][...] - spec) + ins[1][1] * ins[3][...])
        x_inverse(tab, spec, None, outs[0], 0, 1)

    (sent,) = run(staged, twelfth, x_both, (arrived, waves, cot_spec, elev_cot_spec), (message(1),), 1)
    square_fourth_spec, square_cot_spec, cube_cot_spec = run(
        staged, spectra_of((1, 2, 3), 4), x_in, (arrived, waves), (spectrum_shape,) * 3, 1
    )
    arrived = exchange(sent)

    def thirteenth(tab, ins, outs, emit):
        lifted = y_inverse(tab, ins[0], 0, 1)
        outs[1][...] = lifted
        emit(1)
        y_forward(tab, ins[1][...] * lifted, outs[0], 0, 4)
        for slot in range(1, 4):
            put(outs[0], ins[1 + slot][...], slot, 4)

    sent, third_cot = run(
        staged, thirteenth,
        y_both,
        (arrived, elev, cube_fourth_sent, slope_x_cot, slope_y_cot),
        (message(4), field_shape),
        2,
    )
    (square_third_sent,) = sends_of(square * third_cot)
    arrived = exchange(sent)

    def fourteenth(tab, ins, outs, emit):
        wave = ins[1][1]
        spec = x_forward(tab, ins[0], 0, 4) * ins[1][0]
        spec = wave * (
            (ins[2][...] - spec) + wave * ((ins[3][...] - ins[4][...]) + wave * ins[5][...])
        )
        x_inverse(tab, spec, None, outs[0], 0, 1)

    (sent,) = run(
        staged, fourteenth,
        x_both,
        (arrived, waves, cot_spec, elev_cot_spec, square_fourth_spec, square_cot_spec),
        (message(1),),
        1,
    )

    def gathered(tab, ins, outs, emit):
        wave = ins[1][1]
        cube_fourth = x_forward(tab, ins[0], 1, 4) * ins[1][0]
        outs[0][...] = wave * (
            ins[2][...]
            + wave * (ins[3][...] + wave * ((ins[4][...] - cube_fourth) + wave * ins[5][...]))
        )
        slope_x_spec = x_forward(tab, ins[0], 2, 4) * ins[1][0]
        slope_y_spec = x_forward(tab, ins[0], 3, 4) * ins[1][0]
        outs[1][...] = -(ins[7][0] * slope_x_spec + ins[7][1] * slope_y_spec)
        outs[2][...] = ins[6][...] * (wave * wave) * (wave * wave)

    pot_part, elev_turn, elev_part = run(
        staged, gathered,
        x_in,
        (arrived, waves, cot_spec, elev_cot_spec, square_cot_spec, cube_cot_spec, bend_spec, turns),
        (spectrum_shape,) * 3,
        1,
    )
    arrived = exchange(sent)

    def fifteenth(tab, ins, outs, emit):
        lifted = y_inverse(tab, ins[0], 0, 1)
        outs[1][...] = lifted
        emit(1)
        y_forward(tab, ins[1][...] * lifted, outs[0], 0, 4)
        for slot in range(1, 4):
            put(outs[0], ins[1 + slot][...], slot, 4)

    sent, second_cot = run(
        staged, fifteenth,
        y_both,
        (arrived, elev, square_third_sent, flow_x_cot, flow_y_cot),
        (message(4), field_shape),
        2,
    )
    arrived = exchange(sent)

    def elevation_side(tab, ins, outs, emit):
        x_inverse(tab, ins[0][...], ins[1][...], outs[0], 0, 1)

    (elev_sent,) = run(staged, elevation_side, x_out, (elev_part, elev_turn), (part_shape,), 1)

    def sixteenth(tab, ins, outs, emit):
        wave = ins[1][1]
        keep = ins[1][0]
        first_part = x_forward(tab, ins[0], 0, 4) * keep
        second_part = x_forward(tab, ins[0], 1, 4) * keep
        flow_part = x_forward(tab, ins[0], 2, 4) * ins[4][0] + x_forward(tab, ins[0], 3, 4) * ins[4][1]
        straight = ins[2][...] - wave * (first_part + wave * second_part)
        x_inverse(tab, straight, -flow_part * keep, outs[0], 1, 2)
        put(outs[0], ins[3][...], 0, 2)

    (sent,) = run(staged, sixteenth, x_all, (arrived, waves, pot_part, elev_sent, turns), (message(2),), 2)
    arrived = exchange(sent)

    grad = (
        vertical_cot * growth
        - (lift_31 + elev * lift_22 + square * lift_13) * fourth_cot
        - (lift_21 + elev * lift_12) * third_cot
        - lift_11 * second_cot
        - rate_pot
    )

    def finish(tab, ins, outs, emit):
        scatter_rows(outs[1], y_inverse(tab, ins[0], 1, 2), ins[3])
        emit(1)
        scatter_rows(outs[0], ins[1][...] + y_inverse(tab, ins[0], 0, 2), ins[2])

    block = pltpu.HBM(elevation.shape, jnp.float32)
    elevation_grad, potential_grad = run(
        staged, finish, y_out, (arrived, grad, elevation_cot, potential_cot), (block, block), 2
    )
    return (elevation_grad, potential_grad)


def solution(mesh):
    spec = P(mesh_axes, None)
    return jax.shard_map(
        per_device, mesh=mesh, in_specs=(spec,) * 4, out_specs=(spec, spec), check_vma=False
    )
```

```python
import functools

import jax
import jax.numpy as jnp
import numpy as np
from jax import lax
from jax.experimental import pallas as pl
from jax.experimental.pallas import tpu as pltpu
from jax.sharding import PartitionSpec as P

stiffness = 0.05
section_step = 0.25
side = 4096
devices = 256
local_rows = 16
radix = 16
fine = 256
kept_y = 64
kept_a = np.array([0, 1, 2, 3, 12, 13, 14, 15])
mesh_axes = ("rows", "cols")


def split_table(table):
    table = table.astype(np.float32)
    high = table.astype(jnp.bfloat16)
    low = (table - high.astype(np.float32)).astype(jnp.bfloat16)
    return np.stack((high, low), 0)


@functools.lru_cache(maxsize=None)
def tables():
    two_pi = 2.0 * np.pi
    eye_j = np.eye(local_rows)
    residue = np.arange(radix)
    angle = two_pi * np.outer(np.arange(radix), residue) / radix
    parts = np.stack((np.cos(angle), -np.sin(angle)), 0).reshape(2, radix, 4, 4)
    right_y = np.einsum("cthl,jk->tjhckl", parts, eye_j).reshape(radix * local_rows, 512)
    angle = two_pi * np.outer(np.arange(fine), residue) / side
    cosine = np.cos(angle).reshape(fine, 4, 1, 1, 4)
    sine = np.sin(angle).reshape(fine, 4, 1, 1, 4)
    signs = np.array([1.0, -1.0]).reshape(1, 1, 2, 1, 1)
    full = (fine, 4, 2, local_rows, 4)
    twist_y = np.stack(
        (np.broadcast_to(cosine, full).reshape(fine, 512), np.broadcast_to(sine * signs, full).reshape(fine, 512)), 0
    )
    angle = two_pi * np.outer(np.arange(kept_y), np.arange(fine)) / fine
    left_y = np.concatenate((np.cos(angle), np.sin(angle)), 0)
    left_y_back = left_y.T
    angle = two_pi * np.outer(np.arange(fine), np.arange(fine)) / fine
    left_x = np.concatenate((np.cos(angle), np.sin(angle)), 0)
    angle = two_pi * np.outer(np.arange(fine), np.arange(local_rows)) / side
    full = (fine, 2, local_rows, 4)
    signs = np.array([1.0, -1.0]).reshape(1, 2, 1, 1)
    twist_x = np.stack(
        (
            np.broadcast_to(np.cos(angle)[:, None, :, None], full).reshape(fine, 128),
            np.broadcast_to(np.sin(angle)[:, None, :, None] * signs, full).reshape(fine, 128),
        ),
        0,
    )
    angle = two_pi * np.outer(np.arange(local_rows), kept_a) / radix
    cosine, sine = (np.cos(angle), np.sin(angle))
    eye_q = np.eye(4)
    forward = np.array([[cosine, -sine], [sine, cosine]])
    right_x = np.einsum("cdja,qp->cjqdap", forward, eye_q).reshape(128, 64)
    turned = np.array([[-sine, cosine], [-cosine, -sine]])
    right_x_back = right_x.T
    right_x_turn = np.einsum("cdja,qp->caqdjp", turned, eye_q).reshape(64, 128)
    return dict(
        right_y=split_table(right_y),
        right_y_back=split_table(right_y.T),
        left_y=split_table(left_y),
        left_y_back=split_table(left_y_back),
        twist_y=twist_y.astype(np.float32),
        left_x=split_table(left_x),
        right_x=split_table(right_x),
        right_x_back=split_table(right_x_back),
        right_x_turn=split_table(right_x_turn),
        twist_x=twist_x.astype(np.float32),
    )


y_in = ("right_y", "twist_y", "left_y")
y_out = ("left_y_back", "twist_y", "right_y_back")
y_both = ("left_y_back", "twist_y", "right_y_back", "right_y", "left_y")
x_in = ("left_x", "twist_x", "right_x")
x_out = ("right_x_back", "right_x_turn", "twist_x", "left_x")
x_both = ("left_x", "twist_x", "right_x", "right_x_back")
x_turn = ("left_x", "twist_x", "right_x", "right_x_turn")
x_all = ("left_x", "twist_x", "right_x", "right_x_back", "right_x_turn")


def parted(values):
    high = values.astype(jnp.bfloat16)
    return (high, (values - high.astype(jnp.float32)).astype(jnp.bfloat16))


def product(first, second):
    return jnp.dot(first, second, preferred_element_type=jnp.float32)


def left_times(table_ref, values):
    high, low = parted(values)
    return product(table_ref[0], high) + (product(table_ref[1], high) + product(table_ref[0], low))


def times_right(values, table_ref):
    high, low = parted(values)
    return product(high, table_ref[0]) + (product(low, table_ref[0]) + product(high, table_ref[1]))


def swapped(values):
    pieces = [
        pltpu.roll(values[:, start : start + 128], 64, 1) for start in range(0, values.shape[1], 128)
    ]
    return pieces[0] if len(pieces) == 1 else jnp.concatenate(pieces, 1)


def half_signs(shape):
    lane = lax.broadcasted_iota(jnp.int32, shape, 1)
    return jnp.where(lane % 128 < 64, 1.0, -1.0).astype(jnp.float32)


def y_forward(tab, field, message_ref, slot, count):
    values = times_right(field, tab["right_y"])
    values = values * tab["twist_y"][0] + swapped(values) * tab["twist_y"][1]
    both = left_times(tab["left_y"], values)
    turned = swapped(both[kept_y:])
    values = both[:kept_y] + turned * half_signs(turned.shape)
    for part in range(4):
        message_ref[pl.ds(part * count + slot, kept_y, stride=4 * count), :] = values[
            :, part * 128 : part * 128 + 128
        ]


def y_inverse(tab, arrived_ref, slot, count):
    values = jnp.concatenate(
        [arrived_ref[pl.ds(part * count + slot, kept_y, stride=4 * count), :] for part in range(4)], 1
    )
    turned = swapped(values)
    stacked = jnp.concatenate((values, turned * -half_signs(turned.shape)), 0)
    values = left_times(tab["left_y_back"], stacked)
    values = values * tab["twist_y"][0] - swapped(values) * tab["twist_y"][1]
    return times_right(values, tab["right_y_back"])


def x_forward(tab, arrived_ref, slot, count):
    values = arrived_ref[pl.ds(slot, fine, stride=count), :] if count > 1 else arrived_ref[...]
    both = left_times(tab["left_x"], values)
    turned = swapped(both[fine:])
    values = both[:fine] + turned * half_signs(turned.shape)
    values = values * tab["twist_x"][0] + swapped(values) * tab["twist_x"][1]
    return times_right(values, tab["right_x"])


def x_inverse(tab, straight, turned_part, message_ref, slot, count):
    if straight is None:
        values = times_right(turned_part, tab["right_x_turn"])
    else:
        values = times_right(straight, tab["right_x_back"])
        if turned_part is not None:
            values = values + times_right(turned_part, tab["right_x_turn"])
    values = values * tab["twist_x"][0] - swapped(values) * tab["twist_x"][1]
    both = left_times(tab["left_x"], values)
    turned = swapped(both[fine:])
    values = both[:fine] - turned * half_signs(turned.shape)
    put(message_ref, values, slot, count)


def put(message_ref, values, slot, count):
    if count > 1:
        message_ref[pl.ds(slot, fine, stride=count), :] = values
    else:
        message_ref[...] = values


def message(count):
    return pltpu.HBM((devices * count, 128), jnp.float32)


part_shape = pltpu.HBM((devices, 128), jnp.float32)
field_shape = pltpu.HBM((256, 256), jnp.float32)
spectrum_shape = pltpu.HBM((fine, 64), jnp.float32)


class Fetched:
    def __init__(self, source, target, semaphore):
        self.target = target
        self.copy = pltpu.make_async_copy(source, target, semaphore)
        self.copy.start()
        self.pending = True

    def arrive(self):
        if self.pending:
            self.copy.wait()
            self.pending = False

    def __getitem__(self, index):
        self.arrive()
        return self.target[index]


def is_near(shape):
    return shape.memory_space == pltpu.VMEM


resident_names = ("left_x", "twist_x", "right_x", "right_x_back", "twist_y", "left_y_back")


def stage_tables():
    names = resident_names
    values = [pltpu.with_memory_space_constraint(jnp.asarray(tables()[name]), pltpu.HBM) for name in names]
    count = len(values)

    def kernel(*refs):
        copies = [
            pltpu.make_async_copy(refs[i], refs[count + i], refs[-1].at[i]) for i in range(count)
        ]
        for copy in copies:
            copy.start()
        for copy in copies:
            copy.wait()

    staged = pl.pallas_call(
        kernel,
        out_shape=[pltpu.VMEM(a.shape, a.dtype) for a in values],
        in_specs=[pl.BlockSpec(memory_space=pltpu.HBM)] * count,
        out_specs=[pl.BlockSpec(memory_space=pltpu.VMEM)] * count,
        scratch_shapes=[pltpu.SemaphoreType.DMA((count,))],
        compiler_params=pltpu.CompilerParams(vmem_limit_bytes=vmem_limit),
        cost_estimate=pl.CostEstimate(flops=0, bytes_accessed=8_000_000, transcendentals=0),
    )(*values)
    return dict(zip(names, staged))


vmem_limit = 24_000_000


def run(staged, body, names, inputs, outputs, flops):
    staged = staged or {}
    operands = [inputs[0]] + [
        staged[name] if name in staged else jnp.asarray(tables()[name]) for name in names
    ]
    operands = operands + list(inputs[1:])
    near = {1 + place for place, name in enumerate(names) if name in staged}
    near = near | ({0} if inputs[0].shape[1] == 128 and inputs[0].shape[0] < 2048 else set())
    far = set(range(len(operands))) - near
    operands = [
        pltpu.with_memory_space_constraint(a, pltpu.HBM if place in far else pltpu.VMEM)
        for place, a in enumerate(operands)
    ]
    total_in = len(operands)
    total = total_in + len(outputs)
    moving = sorted(far)
    leaving = [place for place, shape in enumerate(outputs) if not is_near(shape)]

    def kernel(*refs):
        semaphores = refs[-1]
        held = refs[total:-1]
        fetched = list(refs[:total_in])
        for slot, place in enumerate(moving):
            fetched[place] = Fetched(refs[place], held[slot], semaphores.at[place])
        tab = dict(zip(names, fetched[1 : 1 + len(names)]))
        ins = fetched[:1] + fetched[1 + len(names) :]
        outs = list(refs[total_in:total])
        for slot, place in enumerate(leaving):
            outs[place] = held[len(moving) + slot]
        sends = {}

        def emit(place):
            if place in leaving:
                copy = pltpu.make_async_copy(
                    outs[place], refs[total_in + place], semaphores.at[total_in + place]
                )
                copy.start()
                sends[place] = copy

        body(tab, ins, outs, emit)
        for place in range(len(outs)):
            if place not in sends:
                emit(place)
        for place in moving:
            fetched[place].arrive()
        for copy in sends.values():
            copy.wait()

    outside = pl.BlockSpec(memory_space=pltpu.HBM)
    inside = pl.BlockSpec(memory_space=pltpu.VMEM)
    moved = sum(4 * int(np.prod(a.shape)) for a in list(operands) + list(outputs))
    scratch = [operands[place] for place in moving] + [outputs[place] for place in leaving]
    return pl.pallas_call(
        kernel,
        out_shape=list(outputs),
        in_specs=[outside if place in far else inside for place in range(total_in)],
        out_specs=[inside if is_near(shape) else outside for shape in outputs],
        scratch_shapes=[pltpu.VMEM(a.shape, a.dtype) for a in scratch]
        + [pltpu.SemaphoreType.DMA((total,))],
        compiler_params=pltpu.CompilerParams(vmem_limit_bytes=vmem_limit),
        cost_estimate=pl.CostEstimate(flops=int(flops * 6e8), bytes_accessed=int(moved), transcendentals=0),
    )(*operands)


def exchange(values):
    count = values.shape[0] // devices
    values = values.reshape(devices, count, 128)
    values = lax.all_to_all(values, mesh_axes, split_axis=0, concat_axis=0, tiled=True)
    return values.reshape(devices * count, 128)


def gather_rows(block):
    pieces = [block[:, start : start + 256] for start in range(0, side, 256)]
    return jnp.concatenate(pieces, 0).T


def scatter_rows(out_ref, field, extra_ref):
    turned = field.T
    for part in range(radix):
        columns = pl.ds(part * 256, 256)
        out_ref[:, columns] = turned[part * local_rows : (part + 1) * local_rows, :] + extra_ref[:, columns]


def wave_tables():
    own = lax.axis_index("rows") * lax.axis_size("cols") + lax.axis_index("cols")
    lane = jnp.arange(64, dtype=jnp.int32)
    digit = (lane // 4) % 8
    mode_y = 4 * own + lane % 4
    row = jnp.arange(fine, dtype=jnp.int32)
    mode_x = 256 * jnp.where(digit < 4, digit, digit - 8)[None, :] + row[:, None]
    wave_x = (2.0 * jnp.pi / side) * mode_x.astype(jnp.float32)
    wave_y = jnp.broadcast_to(((2.0 * jnp.pi / side) * mode_y.astype(jnp.float32))[None, :], wave_x.shape)
    weight = jnp.where(mode_y == 0, 1.0, 2.0)[None, :] / (side * side)
    keep = jnp.where(jnp.abs(mode_x) < side // 4, weight, 0.0).astype(jnp.float32)
    magnitude = jnp.sqrt(wave_x * wave_x + wave_y * wave_y)
    return (jnp.stack((keep, magnitude), 0), jnp.stack((wave_x, wave_y), 0))


def per_device(elevation, potential, elevation_cot, potential_cot):
    waves, turns = wave_tables()

    def start(tab, ins, outs, emit):
        surface = gather_rows(ins[0][...])
        outs[0][...] = surface
        emit(0)
        y_forward(tab, gather_rows(ins[1][...]), outs[1], 1, 2)
        y_forward(tab, surface, outs[1], 0, 2)

    elev, sent = run(None, start, y_in, (elevation, potential), (field_shape, message(2)), 2)
    first = exchange(sent)
    staged = stage_tables()

    def cotangents(tab, ins, outs, emit):
        outs[0][...] = section_step * gather_rows(ins[0][...])
        rate = section_step * gather_rows(ins[1][...])
        outs[1][...] = rate
        y_forward(tab, -stiffness * rate, outs[2], 0, 1)

    rate_elev, rate_pot, bend_sent = run(
        staged, cotangents, y_in, (elevation_cot, potential_cot), (field_shape, field_shape, part_shape), 1
    )

    def second(tab, ins, outs, emit):
        spec = x_forward(tab, ins[0], 1, 2)
        outs[1][...] = spec * ins[1][0]
        spec = spec * ins[1][0]
        for degree in range(4):
            spec = spec * ins[1][1]
            x_inverse(tab, spec, None, outs[0], degree, 4)

    sent, pot_spec = run(staged, second, x_both, (first, waves), (message(4), spectrum_shape), 2)
    lifts = exchange(sent)

    def slopes(tab, ins, outs, emit):
        spec = x_forward(tab, ins[0], 0, 2) * ins[2][0]
        x_inverse(tab, None, spec * ins[3][0], outs[0], 0, 1)
        x_inverse(tab, None, spec * ins[3][1], outs[1], 0, 1)
        spec = ins[1][...]
        x_inverse(tab, None, spec * ins[3][0], outs[2], 0, 1)
        x_inverse(tab, None, spec * ins[3][1], outs[3], 0, 1)

    slope_x_sent, slope_y_sent, flow_x_sent, flow_y_sent = run(
        staged, slopes, x_turn, (first, pot_spec, waves, turns), (part_shape,) * 4, 2
    )

    def third(tab, ins, outs, emit):
        lifted = y_inverse(tab, ins[0], 0, 4)
        outs[1][...] = lifted
        emit(1)
        y_forward(tab, -ins[1][...] * lifted, outs[0], 0, 1)

    sent, lift_11 = run(staged, third, y_both, (lifts, elev), (message(1), field_shape), 2)
    arrived = exchange(sent)

    def inverse_of(slots, count):
        def body(tab, ins, outs, emit):
            for place, slot in enumerate(slots):
                outs[place][...] = y_inverse(tab, ins[0], slot, count)
                emit(place)

        return body

    lift_12, lift_13, lift_14 = run(staged, inverse_of((1, 2, 3), 4), y_out, (lifts,), (field_shape,) * 3, 3)

    def fourth(tab, ins, outs, emit):
        spec = x_forward(tab, ins[0], 0, 1) * ins[1][0]
        for degree in range(3):
            spec = spec * ins[1][1]
            x_inverse(tab, spec, None, outs[0], degree, 4)
        put(outs[0], ins[2][...], 3, 4)

    (sent,) = run(staged, fourth, x_both, (arrived, waves, slope_x_sent), (message(4),), 2)

    def spectra_of(slots, count):
        def body(tab, ins, outs, emit):
            for place, slot in enumerate(slots):
                outs[place][...] = x_forward(tab, ins[0], slot, count) * ins[1][0]

        return body

    arrived = exchange(sent)

    def fifth(tab, ins, outs, emit):
        lifted = y_inverse(tab, ins[0], 0, 4)
        outs[1][...] = lifted
        emit(1)
        surface = ins[1][...]
        y_forward(tab, -surface * lifted - (surface * surface / 2.0) * ins[2][...], outs[0], 0, 1)

    sent, lift_21 = run(staged, fifth, y_both, (arrived, elev, lift_12), (message(1), field_shape), 2)
    lift_22, lift_23, slope_x = run(staged, inverse_of((1, 2, 3), 4), y_out, (arrived,), (field_shape,) * 3, 3)
    arrived = exchange(sent)

    def sixth(tab, ins, outs, emit):
        spec = x_forward(tab, ins[0], 0, 1) * ins[1][0]
        for degree in range(2):
            spec = spec * ins[1][1]
            x_inverse(tab, spec, None, outs[0], degree, 4)
        put(outs[0], ins[2][...], 2, 4)
        put(outs[0], ins[3][...], 3, 4)

    (sent,) = run(staged, sixth, x_both, (arrived, waves, slope_y_sent, flow_x_sent), (message(4),), 2)
    arrived = exchange(sent)

    def seventh(tab, ins, outs, emit):
        lifted = y_inverse(tab, ins[0], 0, 4)
        outs[1][...] = lifted
        emit(1)
        surface = ins[1][...]
        square = surface * surface / 2.0
        cube = square * surface / 3.0
        y_forward(tab, -surface * lifted - square * ins[2][...] - cube * ins[3][...], outs[0], 0, 1)

    sent, lift_31 = run(staged, seventh, y_both, (arrived, elev, lift_22, lift_13), (message(1), field_shape), 2)
    lift_32, slope_y, flow_x = run(staged, inverse_of((1, 2, 3), 4), y_out, (arrived,), (field_shape,) * 3, 3)
    arrived = exchange(sent)

    def eighth(tab, ins, outs, emit):
        spec = x_forward(tab, ins[0], 0, 1) * (ins[1][0] * ins[1][1])
        x_inverse(tab, spec, None, outs[0], 0, 2)
        put(outs[0], ins[2][...], 1, 2)

    (sent,) = run(staged, eighth, x_both, (arrived, waves, flow_y_sent), (message(2),), 1)
    arrived = exchange(sent)

    square = elev * elev / 2.0
    cube = square * elev / 3.0
    partial = (
        lift_11
        + lift_21
        + lift_31
        + elev * (lift_12 + lift_22 + lift_32)
        + square * (lift_13 + lift_23)
        + cube * lift_14
    )
    growth = lift_12 + lift_22 + lift_32 + elev * (lift_13 + lift_23) + square * lift_14
    steepness = 1.0 + slope_x * slope_x + slope_y * slope_y

    def ninth(tab, ins, outs, emit):
        vertical = ins[1][...] + y_inverse(tab, ins[0], 0, 2)
        vertical_cot = ins[2][...] * (ins[3][...] + vertical * ins[4][...])
        outs[1][...] = vertical
        emit(1)
        outs[2][...] = vertical_cot
        emit(2)
        y_forward(tab, vertical_cot, outs[0], 0, 1)

    sent, vertical, vertical_cot = run(
        staged,
        ninth,
        y_both,
        (arrived, partial, steepness, rate_elev, rate_pot),
        (message(1), field_shape, field_shape),
        2,
    )
    (flow_y,) = run(staged, inverse_of((1,), 2), y_out, (arrived,), (field_shape,), 1)
    arrived = exchange(sent)
    steep_cot = vertical * rate_elev + 0.5 * vertical * vertical * rate_pot

    def forward_all(tab, ins, outs, emit):
        for place in range(len(ins)):
            y_forward(tab, ins[place][...], outs[place], 0, 1)
            emit(place)

    def sends_of(*fields):
        return run(staged, forward_all, y_in, fields, (part_shape,) * len(fields), len(fields))

    elev_cot_sent, square_cot_sent, cube_cot_sent = sends_of(
        elev * vertical_cot, square * vertical_cot, cube * vertical_cot
    )
    slope_x_cot, slope_y_cot = sends_of(
        -flow_x * rate_elev + 2.0 * slope_x * steep_cot, -flow_y * rate_elev + 2.0 * slope_y * steep_cot
    )
    flow_x_cot, flow_y_cot = sends_of(
        -slope_x * rate_elev - flow_x * rate_pot, -slope_y * rate_elev - flow_y * rate_pot
    )

    def tenth(tab, ins, outs, emit):
        spec = x_forward(tab, ins[0], 0, 1) * ins[1][0]
        outs[1][...] = spec
        emit(1)
        x_inverse(tab, spec * ins[1][1], None, outs[0], 0, 1)

    sent, cot_spec = run(staged, tenth, x_both, (arrived, waves), (message(1), spectrum_shape), 1)
    arrived = exchange(sent)

    def eleventh(tab, ins, outs, emit):
        for slot in range(1, 8):
            put(outs[0], ins[1 + slot][...], slot, 8)
        lifted = y_inverse(tab, ins[0], 0, 1)
        outs[1][...] = lifted
        emit(1)
        y_forward(tab, ins[1][...] * lifted, outs[0], 0, 8)

    sent, fourth_cot = run(
        staged,
        eleventh,
        y_both,
        (
            arrived,
            elev,
            elev_cot_sent,
            square_cot_sent,
            cube_cot_sent,
            slope_x_cot,
            slope_y_cot,
            flow_x_cot,
            flow_y_cot,
        ),
        (message(8), field_shape),
        2,
    )
    square_fourth_sent, cube_fourth_sent = sends_of(square * fourth_cot, cube * fourth_cot)
    arrived = exchange(sent)

    def twelfth(tab, ins, outs, emit):
        wave = ins[1][1]
        elev_spec = x_forward(tab, ins[0], 1, 8) * ins[1][0]
        outs[1][...] = elev_spec
        emit(1)
        spec = x_forward(tab, ins[0], 0, 8) * ins[1][0]
        spec = wave * ((ins[2][...] - spec) + wave * elev_spec)
        x_inverse(tab, spec, None, outs[0], 0, 1)

    sent, elev_cot_spec = run(
        staged, twelfth, x_both, (arrived, waves, cot_spec), (message(1), spectrum_shape), 2
    )
    square_cot_spec, cube_cot_spec = run(
        staged, spectra_of((2, 3), 8), x_in, (arrived, waves), (spectrum_shape,) * 2, 1
    )

    def turned_parts(tab, ins, outs, emit):
        for place in range(2):
            along_x = x_forward(tab, ins[0], 4 + 2 * place, 8)
            along_y = x_forward(tab, ins[0], 5 + 2 * place, 8)
            outs[place][...] = -ins[1][0] * (ins[2][0] * along_x + ins[2][1] * along_y)

    elev_turn, flow_turn = run(
        staged, turned_parts, x_in, (arrived, waves, turns), (spectrum_shape,) * 2, 2
    )
    arrived = exchange(sent)

    def thirteenth(tab, ins, outs, emit):
        for slot in range(1, 4):
            put(outs[0], ins[1 + slot][...], slot, 4)
        lifted = y_inverse(tab, ins[0], 0, 1)
        outs[1][...] = lifted
        emit(1)
        y_forward(tab, ins[1][...] * lifted, outs[0], 0, 4)

    sent, third_cot = run(
        staged,
        thirteenth,
        y_both,
        (arrived, elev, square_fourth_sent, cube_fourth_sent, bend_sent),
        (message(4), field_shape),
        2,
    )
    (square_third_sent,) = sends_of(square * third_cot)
    arrived = exchange(sent)

    def fourteenth(tab, ins, outs, emit):
        wave = ins[1][1]
        square_fourth = x_forward(tab, ins[0], 1, 4) * ins[1][0]
        spec = x_forward(tab, ins[0], 0, 4) * ins[1][0]
        spec = wave * (
            (ins[2][...] - spec) + wave * ((ins[3][...] - square_fourth) + wave * ins[4][...])
        )
        x_inverse(tab, spec, None, outs[0], 0, 1)

    (sent,) = run(
        staged,
        fourteenth,
        x_both,
        (arrived, waves, cot_spec, elev_cot_spec, square_cot_spec),
        (message(1),),
        2,
    )

    def gathered(tab, ins, outs, emit):
        wave = ins[1][1]
        cube_fourth = x_forward(tab, ins[0], 2, 4) * ins[1][0]
        outs[0][...] = wave * (
            ins[2][...]
            + wave * (ins[3][...] + wave * ((ins[4][...] - cube_fourth) + wave * ins[5][...]))
        )
        bend_spec = x_forward(tab, ins[0], 3, 4) * ins[1][0]
        outs[1][...] = bend_spec * (wave * wave) * (wave * wave)

    pot_part, elev_part = run(
        staged,
        gathered,
        x_in,
        (arrived, waves, cot_spec, elev_cot_spec, square_cot_spec, cube_cot_spec),
        (spectrum_shape,) * 2,
        1,
    )
    arrived = exchange(sent)

    def fifteenth(tab, ins, outs, emit):
        put(outs[0], ins[2][...], 1, 2)
        lifted = y_inverse(tab, ins[0], 0, 1)
        outs[1][...] = lifted
        emit(1)
        y_forward(tab, ins[1][...] * lifted, outs[0], 0, 2)

    sent, second_cot = run(
        staged, fifteenth, y_both, (arrived, elev, square_third_sent), (message(2), field_shape), 2
    )
    arrived = exchange(sent)

    def elevation_side(tab, ins, outs, emit):
        x_inverse(tab, ins[0][...], ins[1][...], outs[0], 0, 1)

    (elev_sent,) = run(staged, elevation_side, x_out, (elev_part, elev_turn), (part_shape,), 1)

    def sixteenth(tab, ins, outs, emit):
        wave = ins[1][1]
        first_part = x_forward(tab, ins[0], 0, 2) * ins[1][0]
        second_part = x_forward(tab, ins[0], 1, 2) * ins[1][0]
        straight = ins[2][...] - wave * (first_part + wave * second_part)
        x_inverse(tab, straight, ins[4][...], outs[0], 1, 2)
        put(outs[0], ins[3][...], 0, 2)

    (sent,) = run(
        staged, sixteenth, x_all, (arrived, waves, pot_part, elev_sent, flow_turn), (message(2),), 2
    )
    arrived = exchange(sent)

    grad = (
        vertical_cot * growth
        - (lift_31 + elev * lift_22 + square * lift_13) * fourth_cot
        - (lift_21 + elev * lift_12) * third_cot
        - lift_11 * second_cot
        - rate_pot
    )

    def finish(tab, ins, outs, emit):
        scatter_rows(outs[1], y_inverse(tab, ins[0], 1, 2), ins[3])
        emit(1)
        scatter_rows(outs[0], ins[1][...] + y_inverse(tab, ins[0], 0, 2), ins[2])

    block = pltpu.HBM(elevation.shape, jnp.float32)
    elevation_grad, potential_grad = run(
        staged, finish, y_out, (arrived, grad, elevation_cot, potential_cot), (block, block), 2
    )
    return (elevation_grad, potential_grad)


def solution(mesh):
    spec = P(mesh_axes, None)
    return jax.shard_map(
        per_device, mesh=mesh, in_specs=(spec,) * 4, out_specs=(spec, spec), check_vma=False
    )
```

```python
import functools

import jax
import jax.numpy as jnp
import numpy as np
from jax import lax
from jax.experimental import pallas as pl
from jax.experimental.pallas import tpu as pltpu
from jax.sharding import PartitionSpec as P

stiffness = 0.05
section_step = 0.25
side = 4096
devices = 256
local_rows = 16
radix = 16
fine = 256
kept_y = 64
kept_a = np.array([0, 1, 2, 3, 12, 13, 14, 15])
mesh_axes = ("rows", "cols")


def split_table(table):
    table = table.astype(np.float32)
    high = table.astype(jnp.bfloat16)
    low = (table - high.astype(np.float32)).astype(jnp.bfloat16)
    return np.stack((high, low), 0)


@functools.lru_cache(maxsize=None)
def tables():
    two_pi = 2.0 * np.pi
    eye_j = np.eye(local_rows)
    residue = np.arange(radix)
    angle = two_pi * np.outer(np.arange(radix), residue) / radix
    parts = np.stack((np.cos(angle), -np.sin(angle)), 0).reshape(2, radix, 4, 4)
    right_y = np.einsum("cthl,jk->tjhckl", parts, eye_j).reshape(radix * local_rows, 512)
    angle = two_pi * np.outer(np.arange(fine), residue) / side
    cosine = np.cos(angle).reshape(fine, 4, 1, 1, 4)
    sine = np.sin(angle).reshape(fine, 4, 1, 1, 4)
    signs = np.array([1.0, -1.0]).reshape(1, 1, 2, 1, 1)
    full = (fine, 4, 2, local_rows, 4)
    twist_y = np.stack(
        (np.broadcast_to(cosine, full).reshape(fine, 512), np.broadcast_to(sine * signs, full).reshape(fine, 512)), 0
    )
    angle = two_pi * np.outer(np.arange(kept_y), np.arange(fine)) / fine
    left_y = np.concatenate((np.cos(angle), np.sin(angle)), 0)
    left_y_back = left_y.T
    angle = two_pi * np.outer(np.arange(fine), np.arange(fine)) / fine
    left_x = np.concatenate((np.cos(angle), np.sin(angle)), 0)
    angle = two_pi * np.outer(np.arange(fine), np.arange(local_rows)) / side
    full = (fine, 2, local_rows, 4)
    signs = np.array([1.0, -1.0]).reshape(1, 2, 1, 1)
    twist_x = np.stack(
        (
            np.broadcast_to(np.cos(angle)[:, None, :, None], full).reshape(fine, 128),
            np.broadcast_to(np.sin(angle)[:, None, :, None] * signs, full).reshape(fine, 128),
        ),
        0,
    )
    angle = two_pi * np.outer(np.arange(local_rows), kept_a) / radix
    cosine, sine = (np.cos(angle), np.sin(angle))
    eye_q = np.eye(4)
    forward = np.array([[cosine, -sine], [sine, cosine]])
    right_x = np.einsum("cdja,qp->cjqdap", forward, eye_q).reshape(128, 64)
    turned = np.array([[-sine, cosine], [-cosine, -sine]])
    right_x_back = right_x.T
    right_x_turn = np.einsum("cdja,qp->caqdjp", turned, eye_q).reshape(64, 128)
    return dict(
        right_y=split_table(right_y),
        right_y_back=split_table(right_y.T),
        left_y=split_table(left_y),
        left_y_back=split_table(left_y_back),
        twist_y=twist_y.astype(np.float32),
        left_x=split_table(left_x),
        right_x=split_table(right_x),
        right_x_back=split_table(right_x_back),
        right_x_turn=split_table(right_x_turn),
        twist_x=twist_x.astype(np.float32),
    )


y_in = ("right_y", "twist_y", "left_y")
y_out = ("left_y_back", "twist_y", "right_y_back")
y_both = ("left_y_back", "twist_y", "right_y_back", "right_y", "left_y")
x_in = ("left_x", "twist_x", "right_x")
x_out = ("right_x_back", "right_x_turn", "twist_x", "left_x")
x_both = ("left_x", "twist_x", "right_x", "right_x_back")
x_turn = ("left_x", "twist_x", "right_x", "right_x_turn")
x_all = ("left_x", "twist_x", "right_x", "right_x_back", "right_x_turn")


def parted(values):
    high = values.astype(jnp.bfloat16)
    return (high, (values - high.astype(jnp.float32)).astype(jnp.bfloat16))


def product(first, second):
    return jnp.dot(first, second, preferred_element_type=jnp.float32)


def left_times(table_ref, values):
    high, low = parted(values)
    if values.shape[0] == 128:
        wide = jnp.concatenate((table_ref[0], table_ref[1]), 1)
        return product(wide, jnp.concatenate((high, high), 0)) + product(table_ref[0], low)
    if values.shape[1] == 128:
        both = product(table_ref[0], jnp.concatenate((high, low), 1))
        return both[:, :128] + (both[:, 128:] + product(table_ref[1], high))
    return product(table_ref[0], high) + (product(table_ref[1], high) + product(table_ref[0], low))


def times_right(values, table_ref):
    high, low = parted(values)
    if values.shape[1] == 128:
        tall = jnp.concatenate((table_ref[0], table_ref[0]), 0)
        return product(jnp.concatenate((high, low), 1), tall) + product(high, table_ref[1])
    return product(high, table_ref[0]) + (product(low, table_ref[0]) + product(high, table_ref[1]))


def swapped(values):
    pieces = [
        pltpu.roll(values[:, start : start + 128], 64, 1) for start in range(0, values.shape[1], 128)
    ]
    return pieces[0] if len(pieces) == 1 else jnp.concatenate(pieces, 1)


def half_signs(shape):
    lane = lax.broadcasted_iota(jnp.int32, shape, 1)
    return jnp.where(lane % 128 < 64, 1.0, -1.0).astype(jnp.float32)


def y_forward(tab, field, message_ref, slot, count):
    values = times_right(field, tab["right_y"])
    values = values * tab["twist_y"][0] + swapped(values) * tab["twist_y"][1]
    both = left_times(tab["left_y"], values)
    turned = swapped(both[kept_y:])
    values = both[:kept_y] + turned * half_signs(turned.shape)
    for part in range(4):
        message_ref[pl.ds(part * count + slot, kept_y, stride=4 * count), :] = values[
            :, part * 128 : part * 128 + 128
        ]


def y_inverse(tab, arrived_ref, slot, count):
    values = jnp.concatenate(
        [arrived_ref[pl.ds(part * count + slot, kept_y, stride=4 * count), :] for part in range(4)], 1
    )
    turned = swapped(values)
    stacked = jnp.concatenate((values, turned * -half_signs(turned.shape)), 0)
    values = left_times(tab["left_y_back"], stacked)
    values = values * tab["twist_y"][0] - swapped(values) * tab["twist_y"][1]
    return times_right(values, tab["right_y_back"])


def x_forward(tab, arrived_ref, slot, count):
    values = arrived_ref[pl.ds(slot, fine, stride=count), :] if count > 1 else arrived_ref[...]
    both = left_times(tab["left_x"], values)
    turned = swapped(both[fine:])
    values = both[:fine] + turned * half_signs(turned.shape)
    values = values * tab["twist_x"][0] + swapped(values) * tab["twist_x"][1]
    return times_right(values, tab["right_x"])


def x_inverse(tab, straight, turned_part, message_ref, slot, count):
    if straight is None:
        values = times_right(turned_part, tab["right_x_turn"])
    else:
        values = times_right(straight, tab["right_x_back"])
        if turned_part is not None:
            values = values + times_right(turned_part, tab["right_x_turn"])
    values = values * tab["twist_x"][0] - swapped(values) * tab["twist_x"][1]
    both = left_times(tab["left_x"], values)
    turned = swapped(both[fine:])
    values = both[:fine] - turned * half_signs(turned.shape)
    put(message_ref, values, slot, count)


def x_forward_all(tab, arrived_ref, slots, count):
    values = jnp.concatenate([arrived_ref[pl.ds(slot, fine, stride=count), :] for slot in slots], 1)
    both = left_times(tab["left_x"], values)
    turned = swapped(both[fine:])
    values = both[:fine] + turned * half_signs(turned.shape)
    pieces = []
    for start in range(0, 128 * len(slots), 128):
        piece = values[:, start : start + 128]
        pieces.append(piece * tab["twist_x"][0] + swapped(piece) * tab["twist_x"][1])
    rows = times_right(jnp.concatenate(pieces, 0), tab["right_x"])
    return [rows[fine * place : fine * (place + 1)] for place in range(len(slots))]


def raised(spectrum, wave, count):
    powers = []
    for _ in range(count):
        spectrum = spectrum * wave
        powers.append(spectrum)
    return powers


def x_inverse_all(tab, spectra, message_ref, count):
    rows = times_right(jnp.concatenate(spectra, 0), tab["right_x_back"])
    pieces = []
    for place in range(len(spectra)):
        piece = rows[fine * place : fine * (place + 1)]
        pieces.append(piece * tab["twist_x"][0] - swapped(piece) * tab["twist_x"][1])
    both = left_times(tab["left_x"], jnp.concatenate(pieces, 1))
    turned = swapped(both[fine:])
    values = both[:fine] - turned * half_signs(turned.shape)
    for place in range(len(spectra)):
        put(message_ref, values[:, 128 * place : 128 * place + 128], place, count)


def put(message_ref, values, slot, count):
    if count > 1:
        message_ref[pl.ds(slot, fine, stride=count), :] = values
    else:
        message_ref[...] = values


def message(count):
    return pltpu.HBM((devices * count, 128), jnp.float32)


part_shape = pltpu.HBM((devices, 128), jnp.float32)
field_shape = pltpu.HBM((256, 256), jnp.float32)
spectrum_shape = pltpu.HBM((fine, 64), jnp.float32)


class Fetched:
    def __init__(self, source, target, semaphore):
        self.target = target
        self.copy = pltpu.make_async_copy(source, target, semaphore)
        self.copy.start()
        self.pending = True

    def arrive(self):
        if self.pending:
            self.copy.wait()
            self.pending = False

    def __getitem__(self, index):
        self.arrive()
        return self.target[index]


def is_near(shape):
    return shape.memory_space == pltpu.VMEM


resident_names = ("left_x", "twist_x", "right_x", "right_x_back", "twist_y", "left_y_back")


def stage_tables():
    names = resident_names
    values = [pltpu.with_memory_space_constraint(jnp.asarray(tables()[name]), pltpu.HBM) for name in names]
    count = len(values)

    def kernel(*refs):
        copies = [
            pltpu.make_async_copy(refs[i], refs[count + i], refs[-1].at[i]) for i in range(count)
        ]
        for copy in copies:
            copy.start()
        for copy in copies:
            copy.wait()

    staged = pl.pallas_call(
        kernel,
        out_shape=[pltpu.VMEM(a.shape, a.dtype) for a in values],
        in_specs=[pl.BlockSpec(memory_space=pltpu.HBM)] * count,
        out_specs=[pl.BlockSpec(memory_space=pltpu.VMEM)] * count,
        scratch_shapes=[pltpu.SemaphoreType.DMA((count,))],
        compiler_params=pltpu.CompilerParams(vmem_limit_bytes=vmem_limit),
        cost_estimate=pl.CostEstimate(flops=0, bytes_accessed=8_000_000, transcendentals=0),
    )(*values)
    return dict(zip(names, staged))


vmem_limit = 24_000_000


def run(staged, body, names, inputs, outputs, flops):
    staged = staged or {}
    operands = [inputs[0]] + [
        staged[name] if name in staged else jnp.asarray(tables()[name]) for name in names
    ]
    operands = operands + list(inputs[1:])
    near = {1 + place for place, name in enumerate(names) if name in staged}
    near = near | ({0} if inputs[0].shape[1] == 128 else set())
    far = set(range(len(operands))) - near
    operands = [
        pltpu.with_memory_space_constraint(a, pltpu.HBM if place in far else pltpu.VMEM)
        for place, a in enumerate(operands)
    ]
    total_in = len(operands)
    total = total_in + len(outputs)
    moving = sorted(far)
    leaving = [place for place, shape in enumerate(outputs) if not is_near(shape)]

    def kernel(*refs):
        semaphores = refs[-1]
        held = refs[total:-1]
        fetched = list(refs[:total_in])
        for slot, place in enumerate(moving):
            fetched[place] = Fetched(refs[place], held[slot], semaphores.at[place])
        tab = dict(zip(names, fetched[1 : 1 + len(names)]))
        ins = fetched[:1] + fetched[1 + len(names) :]
        outs = list(refs[total_in:total])
        for slot, place in enumerate(leaving):
            outs[place] = held[len(moving) + slot]
        sends = {}

        def emit(place):
            if place in leaving:
                copy = pltpu.make_async_copy(
                    outs[place], refs[total_in + place], semaphores.at[total_in + place]
                )
                copy.start()
                sends[place] = copy

        body(tab, ins, outs, emit)
        for place in range(len(outs)):
            if place not in sends:
                emit(place)
        for place in moving:
            fetched[place].arrive()
        for copy in sends.values():
            copy.wait()

    outside = pl.BlockSpec(memory_space=pltpu.HBM)
    inside = pl.BlockSpec(memory_space=pltpu.VMEM)
    moved = sum(4 * int(np.prod(a.shape)) for a in list(operands) + list(outputs))
    scratch = [operands[place] for place in moving] + [outputs[place] for place in leaving]
    return pl.pallas_call(
        kernel,
        out_shape=list(outputs),
        in_specs=[outside if place in far else inside for place in range(total_in)],
        out_specs=[inside if is_near(shape) else outside for shape in outputs],
        scratch_shapes=[pltpu.VMEM(a.shape, a.dtype) for a in scratch]
        + [pltpu.SemaphoreType.DMA((total,))],
        compiler_params=pltpu.CompilerParams(vmem_limit_bytes=vmem_limit),
        cost_estimate=pl.CostEstimate(flops=int(flops * 6e8), bytes_accessed=int(moved), transcendentals=0),
    )(*operands)


def exchange(values):
    count = values.shape[0] // devices
    values = values.reshape(devices, count, 128)
    values = lax.all_to_all(values, mesh_axes, split_axis=0, concat_axis=0, tiled=True)
    return values.reshape(devices * count, 128)


def gather_rows(block):
    pieces = [block[:, start : start + 256] for start in range(0, side, 256)]
    return jnp.concatenate(pieces, 0).T


def scatter_rows(out_ref, field, extra_ref):
    turned = field.T
    for part in range(radix):
        columns = pl.ds(part * 256, 256)
        out_ref[:, columns] = turned[part * local_rows : (part + 1) * local_rows, :] + extra_ref[:, columns]


def wave_tables():
    own = lax.axis_index("rows") * lax.axis_size("cols") + lax.axis_index("cols")
    lane = jnp.arange(64, dtype=jnp.int32)
    digit = (lane // 4) % 8
    mode_y = 4 * own + lane % 4
    row = jnp.arange(fine, dtype=jnp.int32)
    mode_x = 256 * jnp.where(digit < 4, digit, digit - 8)[None, :] + row[:, None]
    wave_x = (2.0 * jnp.pi / side) * mode_x.astype(jnp.float32)
    wave_y = jnp.broadcast_to(((2.0 * jnp.pi / side) * mode_y.astype(jnp.float32))[None, :], wave_x.shape)
    weight = jnp.where(mode_y == 0, 1.0, 2.0)[None, :] / (side * side)
    keep = jnp.where(jnp.abs(mode_x) < side // 4, weight, 0.0).astype(jnp.float32)
    magnitude = jnp.sqrt(wave_x * wave_x + wave_y * wave_y)
    return (jnp.stack((keep, magnitude), 0), jnp.stack((wave_x, wave_y), 0))


def per_device(elevation, potential, elevation_cot, potential_cot):
    waves, turns = wave_tables()

    def start(tab, ins, outs, emit):
        surface = gather_rows(ins[0][...])
        outs[0][...] = surface
        emit(0)
        y_forward(tab, gather_rows(ins[1][...]), outs[1], 1, 2)
        y_forward(tab, surface, outs[1], 0, 2)

    elev, sent = run(None, start, y_in, (elevation, potential), (field_shape, message(2)), 2)
    first = exchange(sent)
    staged = stage_tables()

    def cotangents(tab, ins, outs, emit):
        outs[0][...] = section_step * gather_rows(ins[0][...])
        rate = section_step * gather_rows(ins[1][...])
        outs[1][...] = rate
        y_forward(tab, -stiffness * rate, outs[2], 0, 1)

    rate_elev, rate_pot, bend_sent = run(
        staged, cotangents, y_in, (elevation_cot, potential_cot), (field_shape, field_shape, part_shape), 1
    )

    def second(tab, ins, outs, emit):
        spec = x_forward(tab, ins[0], 1, 2)
        outs[1][...] = spec * ins[1][0]
        x_inverse_all(tab, raised(spec * ins[1][0], ins[1][1], 4), outs[0], 4)

    sent, pot_spec = run(staged, second, x_both, (first, waves), (message(4), spectrum_shape), 2)
    lifts = exchange(sent)

    def slopes(tab, ins, outs, emit):
        spec = x_forward(tab, ins[0], 0, 2) * ins[2][0]
        x_inverse(tab, None, spec * ins[3][0], outs[0], 0, 1)
        x_inverse(tab, None, spec * ins[3][1], outs[1], 0, 1)
        spec = ins[1][...]
        x_inverse(tab, None, spec * ins[3][0], outs[2], 0, 1)
        x_inverse(tab, None, spec * ins[3][1], outs[3], 0, 1)

    slope_x_sent, slope_y_sent, flow_x_sent, flow_y_sent = run(
        staged, slopes, x_turn, (first, pot_spec, waves, turns), (part_shape,) * 4, 2
    )

    def third(tab, ins, outs, emit):
        lifted = y_inverse(tab, ins[0], 0, 4)
        outs[1][...] = lifted
        emit(1)
        y_forward(tab, -ins[1][...] * lifted, outs[0], 0, 2)
        put(outs[0], ins[2][...], 1, 2)

    sent, lift_11 = run(staged, third, y_both, (lifts, elev, bend_sent), (message(2), field_shape), 2)
    arrived = exchange(sent)

    def inverse_of(slots, count):
        def body(tab, ins, outs, emit):
            for place, slot in enumerate(slots):
                outs[place][...] = y_inverse(tab, ins[0], slot, count)
                emit(place)

        return body

    lift_12, lift_13, lift_14 = run(staged, inverse_of((1, 2, 3), 4), y_out, (lifts,), (field_shape,) * 3, 3)

    def fourth(tab, ins, outs, emit):
        spec = x_forward(tab, ins[0], 0, 2) * ins[1][0]
        x_inverse_all(tab, raised(spec, ins[1][1], 3), outs[0], 4)
        put(outs[0], ins[2][...], 3, 4)

    (sent,) = run(staged, fourth, x_both, (arrived, waves, slope_x_sent), (message(4),), 2)

    def spectra_of(slots, count):
        def body(tab, ins, outs, emit):
            for place, slot in enumerate(slots):
                outs[place][...] = x_forward(tab, ins[0], slot, count) * ins[1][0]

        return body

    (bend_spec,) = run(staged, spectra_of((1,), 2), x_in, (arrived, waves), (spectrum_shape,), 1)
    arrived = exchange(sent)

    def fifth(tab, ins, outs, emit):
        lifted = y_inverse(tab, ins[0], 0, 4)
        outs[1][...] = lifted
        emit(1)
        surface = ins[1][...]
        y_forward(tab, -surface * lifted - (surface * surface / 2.0) * ins[2][...], outs[0], 0, 1)

    sent, lift_21 = run(staged, fifth, y_both, (arrived, elev, lift_12), (message(1), field_shape), 2)
    lift_22, lift_23, slope_x = run(staged, inverse_of((1, 2, 3), 4), y_out, (arrived,), (field_shape,) * 3, 3)
    arrived = exchange(sent)

    def sixth(tab, ins, outs, emit):
        spec = x_forward(tab, ins[0], 0, 1) * ins[1][0]
        x_inverse_all(tab, raised(spec, ins[1][1], 2), outs[0], 4)
        put(outs[0], ins[2][...], 2, 4)
        put(outs[0], ins[3][...], 3, 4)

    (sent,) = run(staged, sixth, x_both, (arrived, waves, slope_y_sent, flow_x_sent), (message(4),), 2)
    arrived = exchange(sent)

    def seventh(tab, ins, outs, emit):
        lifted = y_inverse(tab, ins[0], 0, 4)
        outs[1][...] = lifted
        emit(1)
        surface = ins[1][...]
        square = surface * surface / 2.0
        cube = square * surface / 3.0
        y_forward(tab, -surface * lifted - square * ins[2][...] - cube * ins[3][...], outs[0], 0, 1)

    sent, lift_31 = run(staged, seventh, y_both, (arrived, elev, lift_22, lift_13), (message(1), field_shape), 2)
    lift_32, slope_y, flow_x = run(staged, inverse_of((1, 2, 3), 4), y_out, (arrived,), (field_shape,) * 3, 3)
    arrived = exchange(sent)

    def eighth(tab, ins, outs, emit):
        spec = x_forward(tab, ins[0], 0, 1) * (ins[1][0] * ins[1][1])
        x_inverse(tab, spec, None, outs[0], 0, 2)
        put(outs[0], ins[2][...], 1, 2)

    (sent,) = run(staged, eighth, x_both, (arrived, waves, flow_y_sent), (message(2),), 1)
    arrived = exchange(sent)

    square = elev * elev / 2.0
    cube = square * elev / 3.0
    partial = (
        lift_11
        + lift_21
        + lift_31
        + elev * (lift_12 + lift_22 + lift_32)
        + square * (lift_13 + lift_23)
        + cube * lift_14
    )
    growth = lift_12 + lift_22 + lift_32 + elev * (lift_13 + lift_23) + square * lift_14
    steepness = 1.0 + slope_x * slope_x + slope_y * slope_y

    def ninth(tab, ins, outs, emit):
        vertical = ins[1][...] + y_inverse(tab, ins[0], 0, 2)
        vertical_cot = ins[2][...] * (ins[3][...] + vertical * ins[4][...])
        outs[1][...] = vertical
        emit(1)
        outs[2][...] = vertical_cot
        emit(2)
        y_forward(tab, vertical_cot, outs[0], 0, 2)
        y_forward(tab, ins[5][...] * vertical_cot, outs[0], 1, 2)

    sent, vertical, vertical_cot = run(
        staged, ninth,
        y_both,
        (arrived, partial, steepness, rate_elev, rate_pot, elev),
        (message(2), field_shape, field_shape),
        3,
    )
    (flow_y,) = run(staged, inverse_of((1,), 2), y_out, (arrived,), (field_shape,), 1)
    arrived = exchange(sent)
    steep_cot = vertical * rate_elev + 0.5 * vertical * vertical * rate_pot

    def forward_all(tab, ins, outs, emit):
        for place in range(len(ins)):
            y_forward(tab, ins[place][...], outs[place], 0, 1)
            emit(place)

    def sends_of(*fields):
        return run(staged, forward_all, y_in, fields, (part_shape,) * len(fields), len(fields))

    square_cot_sent, cube_cot_sent = sends_of(square * vertical_cot, cube * vertical_cot)
    slope_x_cot, slope_y_cot = sends_of(
        -flow_x * rate_elev + 2.0 * slope_x * steep_cot, -flow_y * rate_elev + 2.0 * slope_y * steep_cot
    )
    flow_x_cot, flow_y_cot = sends_of(
        -slope_x * rate_elev - flow_x * rate_pot, -slope_y * rate_elev - flow_y * rate_pot
    )

    def tenth(tab, ins, outs, emit):
        spec = x_forward(tab, ins[0], 0, 2) * ins[1][0]
        outs[1][...] = spec
        emit(1)
        x_inverse(tab, spec * ins[1][1], None, outs[0], 0, 1)

    sent, cot_spec = run(staged, tenth, x_both, (arrived, waves), (message(1), spectrum_shape), 1)
    (elev_cot_spec,) = run(staged, spectra_of((1,), 2), x_in, (arrived, waves), (spectrum_shape,), 1)
    arrived = exchange(sent)

    def eleventh(tab, ins, outs, emit):
        lifted = y_inverse(tab, ins[0], 0, 1)
        outs[1][...] = lifted
        emit(1)
        surface = ins[1][...]
        y_forward(tab, surface * lifted, outs[0], 0, 4)
        y_forward(tab, (surface * surface / 2.0) * lifted, outs[0], 1, 4)
        put(outs[0], ins[2][...], 2, 4)
        put(outs[0], ins[3][...], 3, 4)

    sent, fourth_cot = run(
        staged, eleventh, y_both, (arrived, elev, square_cot_sent, cube_cot_sent), (message(4), field_shape), 3
    )
    (cube_fourth_sent,) = sends_of(cube * fourth_cot)
    arrived = exchange(sent)

    def twelfth(tab, ins, outs, emit):
        spec = x_forward(tab, ins[0], 0, 4) * ins[1][0]
        spec = ins[1][1] * ((ins[2][...] - spec) + ins[1][1] * ins[3][...])
        x_inverse(tab, spec, None, outs[0], 0, 1)

    (sent,) = run(staged, twelfth, x_both, (arrived, waves, cot_spec, elev_cot_spec), (message(1),), 1)
    square_fourth_spec, square_cot_spec, cube_cot_spec = run(
        staged, spectra_of((1, 2, 3), 4), x_in, (arrived, waves), (spectrum_shape,) * 3, 1
    )
    arrived = exchange(sent)

    def thirteenth(tab, ins, outs, emit):
        lifted = y_inverse(tab, ins[0], 0, 1)
        outs[1][...] = lifted
        emit(1)
        y_forward(tab, ins[1][...] * lifted, outs[0], 0, 4)
        for slot in range(1, 4):
            put(outs[0], ins[1 + slot][...], slot, 4)

    sent, third_cot = run(
        staged, thirteenth,
        y_both,
        (arrived, elev, cube_fourth_sent, slope_x_cot, slope_y_cot),
        (message(4), field_shape),
        2,
    )
    (square_third_sent,) = sends_of(square * third_cot)
    arrived = exchange(sent)

    def fourteenth(tab, ins, outs, emit):
        wave = ins[1][1]
        spec = x_forward(tab, ins[0], 0, 4) * ins[1][0]
        spec = wave * (
            (ins[2][...] - spec) + wave * ((ins[3][...] - ins[4][...]) + wave * ins[5][...])
        )
        x_inverse(tab, spec, None, outs[0], 0, 1)

    (sent,) = run(
        staged, fourteenth,
        x_both,
        (arrived, waves, cot_spec, elev_cot_spec, square_fourth_spec, square_cot_spec),
        (message(1),),
        1,
    )

    def gathered(tab, ins, outs, emit):
        wave = ins[1][1]
        cube_fourth = x_forward(tab, ins[0], 1, 4) * ins[1][0]
        outs[0][...] = wave * (
            ins[2][...]
            + wave * (ins[3][...] + wave * ((ins[4][...] - cube_fourth) + wave * ins[5][...]))
        )
        slope_x_spec = x_forward(tab, ins[0], 2, 4) * ins[1][0]
        slope_y_spec = x_forward(tab, ins[0], 3, 4) * ins[1][0]
        outs[1][...] = -(ins[7][0] * slope_x_spec + ins[7][1] * slope_y_spec)
        outs[2][...] = ins[6][...] * (wave * wave) * (wave * wave)

    pot_part, elev_turn, elev_part = run(
        staged, gathered,
        x_in,
        (arrived, waves, cot_spec, elev_cot_spec, square_cot_spec, cube_cot_spec, bend_spec, turns),
        (spectrum_shape,) * 3,
        1,
    )
    arrived = exchange(sent)

    def fifteenth(tab, ins, outs, emit):
        lifted = y_inverse(tab, ins[0], 0, 1)
        outs[1][...] = lifted
        emit(1)
        y_forward(tab, ins[1][...] * lifted, outs[0], 0, 4)
        for slot in range(1, 4):
            put(outs[0], ins[1 + slot][...], slot, 4)

    sent, second_cot = run(
        staged, fifteenth,
        y_both,
        (arrived, elev, square_third_sent, flow_x_cot, flow_y_cot),
        (message(4), field_shape),
        2,
    )
    arrived = exchange(sent)

    def elevation_side(tab, ins, outs, emit):
        x_inverse(tab, ins[0][...], ins[1][...], outs[0], 0, 1)

    (elev_sent,) = run(staged, elevation_side, x_out, (elev_part, elev_turn), (part_shape,), 1)

    def sixteenth(tab, ins, outs, emit):
        wave = ins[1][1]
        keep = ins[1][0]
        first_part, second_part, along_x, along_y = x_forward_all(tab, ins[0], (0, 1, 2, 3), 4)
        flow_part = along_x * ins[4][0] + along_y * ins[4][1]
        straight = ins[2][...] - keep * wave * (first_part + wave * second_part)
        x_inverse(tab, straight, -flow_part * keep, outs[0], 1, 2)
        put(outs[0], ins[3][...], 0, 2)

    (sent,) = run(staged, sixteenth, x_all, (arrived, waves, pot_part, elev_sent, turns), (message(2),), 2)
    arrived = exchange(sent)

    grad = (
        vertical_cot * growth
        - (lift_31 + elev * lift_22 + square * lift_13) * fourth_cot
        - (lift_21 + elev * lift_12) * third_cot
        - lift_11 * second_cot
        - rate_pot
    )

    def finish(tab, ins, outs, emit):
        scatter_rows(outs[1], y_inverse(tab, ins[0], 1, 2), ins[3])
        emit(1)
        scatter_rows(outs[0], ins[1][...] + y_inverse(tab, ins[0], 0, 2), ins[2])

    block = pltpu.HBM(elevation.shape, jnp.float32)
    elevation_grad, potential_grad = run(
        staged, finish, y_out, (arrived, grad, elevation_cot, potential_cot), (block, block), 2
    )
    return (elevation_grad, potential_grad)


def solution(mesh):
    spec = P(mesh_axes, None)
    return jax.shard_map(
        per_device, mesh=mesh, in_specs=(spec,) * 4, out_specs=(spec, spec), check_vma=False
    )
```
